32 devices in a mesh: fsdp: 2 (over y), context: 4 (over x, core), tensor: 4 (over z).
Axes of the slice: x: 2, y: 2, z: 4, core: 2. Of those that a mesh axis runs over, the one named last changes fastest.
Arguments:
- hidden_in: bfloat16 [2, 1024, 1024], P('fsdp', 'context'), may hold values from -6 to 6
- segments: int32 [2, 1024], P('fsdp', 'context'), may hold values from 0 to 2, as said below
- routes: int32 [2, 1024, 8], P('fsdp', ('context', 'tensor')), may hold values from 0 to 15, all different within a row; in each aligned block of 64 rows (0 to 63, 64 to 127, ..., all dimensions but the last counted through in order) at most 48 rows name the same one
- attn_gain: bfloat16 [1024], P(('fsdp', 'context')), may hold values from 0.5 to 1.5
- w_query: bfloat16 [1024, 1024], P(('fsdp', 'context'), 'tensor'), may hold values from -0.1875 to 0.1875
- key_projection: bfloat16 [1024, 512], P(('fsdp', 'context'), 'tensor'), may hold values from -0.1875 to 0.1875
- value_projection: bfloat16 [1024, 512], P(('fsdp', 'context'), 'tensor'), may hold values from -0.1875 to 0.1875
- w_out: bfloat16 [1024, 1024], P('tensor', ('fsdp', 'context')), may hold values from -3 to 3
- moe_gain: bfloat16 [1024], P(('fsdp', 'context')), may hold values from 0.5 to 1.5
- w_router: bfloat16 [1024, 16], P(('fsdp', 'context')), may hold values from -0.09375 to 0.09375
- w_gate: bfloat16 [16, 1024, 512], P(('context', 'tensor'), 'fsdp'), may hold values from -0.1875 to 0.1875
- w_up: bfloat16 [16, 1024, 512], P(('context', 'tensor'), 'fsdp'), may hold values from -0.1875 to 0.1875
- w_down: bfloat16 [16, 512, 1024], P(('context', 'tensor'), None, 'fsdp'), may hold values from -1 to 1
- out_grad: bfloat16 [2, 1024, 1024], P('fsdp', ('context', 'tensor')), may hold values from -6 to 6
Outputs:
- block_output: bfloat16 [2, 1024, 1024], P('fsdp', ('context', 'tensor'))
- input_grad: float32 [2, 1024, 1024], P('fsdp', ('context', 'tensor'))
- attn_gain_grad: float32 [1024], P(('fsdp', 'context'))
- query_grad: float32 [1024, 1024], P(('fsdp', 'context'), 'tensor')
- key_grad: float32 [1024, 512], P(('fsdp', 'context'), 'tensor')
- value_grad: float32 [1024, 512], P(('fsdp', 'context'), 'tensor')
- out_proj_grad: float32 [1024, 1024], P('tensor', ('fsdp', 'context'))
- moe_gain_grad: float32 [1024], P(('fsdp', 'context'))
- router_grad: float32 [1024, 16], P(('fsdp', 'context'))
- gate_grad: float32 [16, 1024, 512], P(('context', 'tensor'), 'fsdp')
- up_grad: float32 [16, 1024, 512], P(('context', 'tensor'), 'fsdp')
- down_grad: float32 [16, 512, 1024], P(('context', 'tensor'), None, 'fsdp')
The draws below stay inside these ranges and needn't reach their ends.
Inputs may be any that keep to these rules, and one draw needn't show every extreme that they name: `routes`: each row names 8 different experts; in each aligned block of 64 rows (the tokens of one device) no expert is named by more than 48 rows, a bound that some block reaches. Segment numbers never fall along a sequence; segment 1 begins within the first 256 positions of each sequence and its last position lies within the last 256; segments 0 and 2 are not empty.
All inputs are finite; a program needn't handle non-finite values.
Results may differ from the reference program's by a relative error of at most 0.018.
Values may be sent and summed in bfloat16 or wider, within the bound.
A program may use at most 128 MiB of HBM per device.

```python
import math
import jax
import jax.numpy as jnp
import numpy as np
from jax import lax

MODEL_DIMENSION = 1024
QUERY_HEAD_COUNT = 16
KEY_VALUE_HEADS = 8
HEAD_FEATURES = 64
FF = 512
TOP = 8
SEQ_DEV = 256
EXPERTS = 16
SEQS = 2
SEQ_LEN = 1024
ROWS_Q = 64
CAP = 48


def draw_segments(key, part):
    key = jax.random.fold_in(key, 7)
    first_key, second_key = jax.random.split(key)
    begins = jax.random.randint(first_key, (SEQS, 1), 1, SEQ_DEV)
    finish = jax.random.randint(second_key, (SEQS, 1), SEQ_LEN - SEQ_DEV + 1, SEQ_LEN)
    positions = jnp.arange(SEQ_LEN, dtype=jnp.int32)[None, :]
    return (positions >= begins).astype(jnp.int32) + (positions >= finish).astype(jnp.int32)


def block_levels(stream_key, extent, cuts, smallest, largest):
    def one(dim, blocks):
        heights = jax.random.uniform(jax.random.fold_in(jax.random.fold_in(stream_key, 6), dim), (blocks,), jnp.float32, smallest / len(cuts), largest / len(cuts))
        return jnp.repeat(jnp.exp(heights), extent[dim] // blocks).reshape((-1,) + (1,) * (len(extent) - dim - 1))

    loudness = one(*cuts[0])
    for cut in cuts[1:]:
        loudness = loudness * one(*cut)
    return loudness


def deal_out(rng, own, number, rows, count, top, bound, slope):
    sequence = jax.random.permutation(rng, count)
    crowded, usual = portions_of(count, rows * top, bound, slope, True), portions_of(count, rows * top, bound, slope, False)
    places = jnp.arange(count)

    def named(sizes, rotation):
        used = int((sizes > 0).sum())
        fixed = max(1, used // 4)
        passed = fixed + (places - fixed + rotation * (used - fixed)) % max(1, count - fixed)
        return jnp.zeros((count,), jnp.int32).at[sequence[jnp.where(places < fixed, places, passed)]].set(jnp.asarray(sizes, jnp.int32))

    sizes = jnp.where(number % 4 == 0, named(crowded, number // 4), named(usual, number - number // 4 - 1))
    mixed = jax.random.permutation(jax.random.fold_in(own, 3), count)
    donor, taker = mixed[0:count // 2 * 2:2], mixed[1:count // 2 * 2:2]
    room = jnp.minimum(sizes[donor] - 1, bound - sizes[taker]) // 2
    room = jnp.where((donor == sequence[0]) | (taker == sequence[0]) | (sizes[taker] == 0), 0, jnp.maximum(room, 0))
    passed = jax.random.randint(jax.random.fold_in(own, 4), (count // 2,), 0, 1 << 20) % (room + 1)
    sizes = sizes.at[donor].add(-passed).at[taker].add(passed)
    items = jnp.searchsorted(jnp.cumsum(sizes), jnp.arange(rows * top), side="right").astype(jnp.int32)
    table = items.reshape(top, rows).T
    table = table[jax.random.permutation(jax.random.fold_in(own, 1), rows)]
    rotation = jax.random.randint(jax.random.fold_in(own, 2), (rows, 1), 0, top)
    return jnp.take_along_axis(table, (jnp.arange(top)[None, :] + rotation) % top, axis=1)


def portions_of(number_of, total, bound, skew, full):
    loads = [(1 << 20) // math.isqrt(grade ** skew) + 1 for grade in range(1, number_of + 1)]
    largest = bound if full else min(bound, max(-(-total // number_of), total * loads[0] // sum(loads)))
    least = 1 if total - largest >= number_of - 1 else 0
    given, surplus = [largest] + [least] * (number_of - 1), total - largest - least * (number_of - 1)
    while surplus > 0:
        movable = [i for i in range(1, number_of) if given[i] < largest] or [i for i in range(1, number_of) if given[i] < bound]
        pool, left = sum([loads[i] for i in movable]), surplus
        for i in movable:
            addition = min(bound - given[i], max(1, left * loads[i] // pool), surplus)
            given[i] = given[i] + addition
            surplus = surplus - addition
    return np.array(given)


def bell_draw(rng, extent, scale, limit, shards=(), kind=jnp.bfloat16):
    values = jax.random.normal(rng, extent, jnp.float32) * scale
    if len(shards) > 0:
        values = block_levels(rng, extent, shards, -0.22, 0.18) * values
    return jnp.clip(values, min=-limit, max=limit).astype(kind)


def setup_inputs(seed: int = 0) -> dict:
    key_list = jax.random.split(jax.random.key(seed), 15)
    hidden_in = bell_draw(key_list[0], (SEQS, SEQ_LEN, MODEL_DIMENSION), 1.0, 6.0, ((0, 2), (1, 4)))
    segments = draw_segments(jax.random.fold_in(key_list[14], 71), 0)
    routes_keys = jax.random.split(jax.random.fold_in(key_list[2], 1), SEQS * SEQ_LEN // ROWS_Q)
    routes_turns = jax.random.permutation(jax.random.fold_in(key_list[2], 3), SEQS * SEQ_LEN // ROWS_Q)
    routes = jax.vmap(lambda own, number: deal_out(jax.random.fold_in(key_list[2], 2), own, number, ROWS_Q, EXPERTS, TOP, CAP, 1))(routes_keys, routes_turns).reshape((SEQS, SEQ_LEN, TOP))
    attn_gain = jnp.clip(1.0 + 0.1 * jax.random.normal(key_list[3], (MODEL_DIMENSION,), jnp.float32), 0.5, 1.5).astype(jnp.bfloat16)
    w_query = bell_draw(key_list[4], (MODEL_DIMENSION, QUERY_HEAD_COUNT * HEAD_FEATURES), MODEL_DIMENSION ** -0.5, 0.1875, ((0, 8), (1, 4)))
    key_projection = bell_draw(key_list[5], (MODEL_DIMENSION, KEY_VALUE_HEADS * HEAD_FEATURES), MODEL_DIMENSION ** -0.5, 0.1875, ((0, 8), (1, 4)))
    value_projection = bell_draw(key_list[6], (MODEL_DIMENSION, KEY_VALUE_HEADS * HEAD_FEATURES), MODEL_DIMENSION ** -0.5, 0.1875, ((0, 8), (1, 4)))
    w_out = bell_draw(key_list[7], (QUERY_HEAD_COUNT * HEAD_FEATURES, MODEL_DIMENSION), (max(1, QUERY_HEAD_COUNT * HEAD_FEATURES // 256)) ** -0.5, 3.0, ((0, 4), (1, 8)))
    moe_gain = jnp.clip(1.0 + 0.1 * jax.random.normal(key_list[8], (MODEL_DIMENSION,), jnp.float32), 0.5, 1.5).astype(jnp.bfloat16)
    w_router = bell_draw(key_list[9], (MODEL_DIMENSION, EXPERTS), (4 * MODEL_DIMENSION) ** -0.5, 0.09375, ((0, 8),))
    w_gate = bell_draw(key_list[10], (EXPERTS, MODEL_DIMENSION, FF), MODEL_DIMENSION ** -0.5, 0.1875, ((0, 16), (1, 2)))
    w_up = bell_draw(key_list[11], (EXPERTS, MODEL_DIMENSION, FF), MODEL_DIMENSION ** -0.5, 0.1875, ((0, 16), (1, 2)))
    w_down = bell_draw(key_list[12], (EXPERTS, FF, MODEL_DIMENSION), (FF // 16) ** -0.5, 1.0, ((0, 16), (2, 2)))
    out_grad = bell_draw(key_list[13], (SEQS, SEQ_LEN, MODEL_DIMENSION), 1.0, 6.0, ((0, 2), (1, 16)))
    return dict(hidden_in=hidden_in, segments=segments, routes=routes, attn_gain=attn_gain, w_query=w_query, key_projection=key_projection, value_projection=value_projection, w_out=w_out, moe_gain=moe_gain, w_router=w_router, w_gate=w_gate, w_up=w_up, w_down=w_down, out_grad=out_grad)


@jax.custom_vjp
def lower_precision(v):
    return lax.optimization_barrier(v.astype(jnp.bfloat16)).astype(jnp.float32)

@jax.custom_vjp
def lower_precision_backward(v):
    return v

def low_keep(v):
    return (lower_precision(v), None)

def low_pass(kept, grad):
    return (grad,)

def back_keep(v):
    return (v, None)

def back_low(kept, grad):
    return (lower_precision(grad),)
lower_precision.defvjp(low_keep, low_pass)
lower_precision_backward.defvjp(back_keep, back_low)
rope_base = 10000.0
norm_eps = 1e-06
highest_precision = lax.Precision.HIGHEST

def norm_scale(values):
    return lax.rsqrt(lax.optimization_barrier(jnp.mean(values * values, axis=-1, keepdims=True)) + norm_eps)

def rope_tables(positions):
    half_dim = HEAD_FEATURES // 2
    frequency = rope_base ** (-(2.0 * jnp.arange(half_dim, dtype=jnp.float32)) / HEAD_FEATURES)
    angles = positions.astype(jnp.float32)[:, None] * frequency[None, :]
    return (jnp.cos(angles), jnp.sin(angles))

def rotate(vectors, cos_table, sin_table):
    half_dim = HEAD_FEATURES // 2
    first_half = vectors[..., :half_dim]
    second_half = vectors[..., half_dim:]
    cos_wide = cos_table[:, None, :]
    sin_wide = sin_table[:, None, :]
    return jnp.concatenate([first_half * cos_wide - second_half * sin_wide, second_half * cos_wide + first_half * sin_wide], axis=-1)

def attention_branch(normed_input, seg_row, w_query, key_projection, value_projection, w_out):
    sequence_length = normed_input.shape[0]
    positions = jnp.arange(sequence_length, dtype=jnp.int32)
    cos_table, sin_table = rope_tables(positions)
    query_rows_projected = lower_precision_backward(jnp.dot(normed_input, w_query, precision=highest_precision)).reshape(sequence_length, QUERY_HEAD_COUNT, HEAD_FEATURES)
    projected_key_rows = lower_precision_backward(jnp.dot(normed_input, key_projection, precision=highest_precision)).reshape(sequence_length, KEY_VALUE_HEADS, HEAD_FEATURES)
    projected_value_rows = lower_precision(lower_precision_backward(jnp.dot(normed_input, value_projection, precision=highest_precision))).reshape(sequence_length, KEY_VALUE_HEADS, HEAD_FEATURES)
    query_rows_projected = lower_precision(rotate(query_rows_projected, cos_table, sin_table) * HEAD_FEATURES ** (-0.5))
    projected_key_rows = lower_precision(rotate(projected_key_rows, cos_table, sin_table))
    grouped_queries = query_rows_projected.reshape(sequence_length, KEY_VALUE_HEADS, QUERY_HEAD_COUNT // KEY_VALUE_HEADS, HEAD_FEATURES)
    scores = lower_precision_backward(jnp.einsum('rkgd,lkd->kgrl', grouped_queries, projected_key_rows, precision=highest_precision))
    allowed = (positions[None, :] <= positions[:, None]) & (seg_row[None, :] == seg_row[:, None])
    scores = jnp.where(allowed, scores, -jnp.inf)
    top_score = lax.optimization_barrier(jnp.max(scores, axis=-1, keepdims=True))
    raised = jnp.exp(scores - top_score)
    prob_low = lower_precision(raised / lax.optimization_barrier(jnp.sum(raised, axis=-1, keepdims=True)))
    mixed_heads = jnp.einsum('kgrl,lkd->rkgd', prob_low, projected_value_rows, precision=highest_precision)
    mixed_heads = lower_precision(lower_precision_backward(mixed_heads)).reshape(sequence_length, QUERY_HEAD_COUNT * HEAD_FEATURES)
    return lower_precision_backward(jnp.dot(mixed_heads, w_out, precision=highest_precision))

def dispatch_tables(route_row):
    sequence_length = route_row.shape[0]
    block_count = sequence_length // ROWS_Q
    route_hits = lax.optimization_barrier(jnp.sum((route_row[:, :, None] == jnp.arange(EXPERTS, dtype=jnp.int32)[None, None, :]).astype(jnp.int32), axis=1, dtype=jnp.int32))
    blocked = route_hits.reshape(block_count, ROWS_Q, EXPERTS)
    slot_rows = jnp.cumsum(blocked, axis=1, dtype=jnp.int32) - 1
    slot_index = jnp.where(blocked > 0, slot_rows, CAP)
    expert_index = jnp.broadcast_to(jnp.arange(EXPERTS, dtype=jnp.int32)[None, None, :], blocked.shape)
    block_index = jnp.broadcast_to(jnp.arange(block_count, dtype=jnp.int32)[:, None, None], blocked.shape)
    token_index = jnp.broadcast_to(jnp.arange(sequence_length, dtype=jnp.int32).reshape(block_count, ROWS_Q, 1), blocked.shape)
    token_ids = jnp.full((EXPERTS, block_count, CAP), sequence_length, jnp.int32)
    token_ids = token_ids.at[expert_index, block_index, slot_index].set(token_index, mode='drop')
    slot_pick = jnp.take_along_axis(slot_rows.reshape(sequence_length, EXPERTS), route_row, axis=1)
    return (token_ids, slot_pick)

def expert_branch(normed_two, route_row, w_router, w_gate, w_up, w_down):
    sequence_length = normed_two.shape[0]
    logits = lower_precision_backward(jnp.dot(normed_two, w_router, precision=highest_precision))
    chosen = jnp.take_along_axis(logits, route_row, axis=1)
    top_logit = lax.optimization_barrier(jnp.max(chosen, axis=-1, keepdims=True))
    raised = jnp.exp(chosen - top_logit)
    gate_probs = raised / lax.optimization_barrier(jnp.sum(raised, axis=-1, keepdims=True))
    token_ids, slot_pick = dispatch_tables(route_row)
    padded = jnp.concatenate([normed_two, jnp.zeros((1, normed_two.shape[1]), jnp.float32)], axis=0)
    dispatched = lower_precision_backward(padded[token_ids])
    gate_pre = lower_precision_backward(jnp.einsum('ebcd,edf->ebcf', dispatched, w_gate, precision=highest_precision))
    up_pre = lower_precision_backward(jnp.einsum('ebcd,edf->ebcf', dispatched, w_up, precision=highest_precision))
    activated = lower_precision(gate_pre * jax.nn.sigmoid(gate_pre) * up_pre)
    expert_out = lower_precision(lower_precision_backward(jnp.einsum('ebcf,efd->ebcd', activated, w_down, precision=highest_precision)))
    blocks = jnp.arange(sequence_length, dtype=jnp.int32) // ROWS_Q
    picked = expert_out[route_row, blocks[:, None], slot_pick]
    return lax.optimization_barrier(jnp.sum(gate_probs[:, :, None] * picked, axis=1))

def block_forward(hidden_seq, seg_row, route_row, params):
    attn_gain, w_query, key_projection, value_projection, w_out, moe_gain, w_router, w_gate, w_up, w_down = params
    normed_input = lower_precision(hidden_seq * norm_scale(hidden_seq) * attn_gain)
    residual = hidden_seq + attention_branch(normed_input, seg_row, w_query, key_projection, value_projection, w_out)
    normed_two = lower_precision(residual * norm_scale(residual) * moe_gain)
    return residual + expert_branch(normed_two, route_row, w_router, w_gate, w_up, w_down)

def reference(hidden_in, segments, routes, attn_gain, w_query, key_projection, value_projection, w_out, moe_gain, w_router, w_gate, w_up, w_down, out_grad):
    params = (attn_gain.astype(jnp.float32), w_query.astype(jnp.float32), key_projection.astype(jnp.float32), value_projection.astype(jnp.float32), w_out.astype(jnp.float32), moe_gain.astype(jnp.float32), w_router.astype(jnp.float32), w_gate.astype(jnp.float32), w_up.astype(jnp.float32), w_down.astype(jnp.float32))
    hidden = hidden_in.astype(jnp.float32)
    checked = jax.checkpoint(block_forward)

    def forward(hidden_all, param_set):

        def one_sequence(carried, seq_inputs):
            return (carried, checked(seq_inputs[0], seq_inputs[1], seq_inputs[2], param_set))
        unused, result = lax.scan(one_sequence, jnp.zeros((), jnp.float32), (hidden_all, segments, routes))
        return result
    result, pullback = jax.vjp(forward, hidden, params)
    input_grad, param_grads = pullback(out_grad.astype(jnp.float32))
    return (result.astype(jnp.bfloat16), input_grad, param_grads[0], param_grads[1], param_grads[2], param_grads[3], param_grads[4], param_grads[5], param_grads[6], param_grads[7], param_grads[8], param_grads[9])
```

```python
import functools

import jax
import jax.numpy as jnp
from jax import lax
from jax.experimental import pallas as pl
from jax.experimental.pallas import tpu as pltpu
from jax.sharding import PartitionSpec as P

HEAD_FEATURES = 64
rope_base = 10000.0
norm_eps = 1e-06
MESH = pl.DeviceIdType.MESH
VMEM_LIMIT = 48 * 1024 * 1024


def wrap(value, size):
    return lax.rem(value + size, size)


def greet(devices):
    barrier = pltpu.get_barrier_semaphore()
    for device in devices:
        pl.semaphore_signal(barrier, inc=1, device_id=device, device_id_type=MESH)
    pl.semaphore_wait(barrier, len(devices))


def send(source, target, send_sem, recv_sem, device):
    copy = pltpu.make_async_remote_copy(
        src_ref=source,
        dst_ref=target,
        send_sem=send_sem,
        recv_sem=recv_sem,
        device_id=device,
        device_id_type=MESH,
    )
    copy.start()
    return copy


def axis_gather_kernel(axis, size, x_ref, o_ref, send_sem, recv_sem, own_sem):
    me = lax.axis_index(axis)
    peers = [{axis: wrap(me + k, size)} for k in range(1, size)]
    greet(peers)
    copies = [
        send(x_ref, o_ref.at[me], send_sem.at[k], recv_sem.at[k], peers[k]) for k in range(size - 1)
    ]
    own = pltpu.make_async_copy(x_ref, o_ref.at[me], own_sem)
    own.start()
    own.wait()
    for copy in copies:
        copy.wait()


def axis_gather(x, axis, number):
    size = lax.axis_size(axis)
    return pl.pallas_call(
        functools.partial(axis_gather_kernel, axis, size),
        out_shape=jax.ShapeDtypeStruct((size,) + x.shape, x.dtype),
        in_specs=[pl.BlockSpec(memory_space=pltpu.VMEM)],
        out_specs=pl.BlockSpec(memory_space=pltpu.VMEM),
        scratch_shapes=[
            pltpu.SemaphoreType.DMA((size - 1,)),
            pltpu.SemaphoreType.DMA((size - 1,)),
            pltpu.SemaphoreType.DMA,
        ],
        compiler_params=pltpu.CompilerParams(
            collective_id=number, has_side_effects=True, vmem_limit_bytes=VMEM_LIMIT
        ),
        name="axis_gather_%d" % number,
    )(x)


def axis_scatter_kernel(axis, size, x_ref, o_ref, held, send_sem, recv_sem):
    me = lax.axis_index(axis)
    places = [wrap(me + k, size) for k in range(1, size)]
    greet([{axis: place} for place in places])
    copies = [
        send(x_ref.at[places[k]], held.at[k], send_sem.at[k], recv_sem.at[k], {axis: places[k]})
        for k in range(size - 1)
    ]
    for copy in copies:
        copy.wait()
    total = x_ref[me].astype(jnp.float32)
    for k in range(size - 1):
        total = total + held[k].astype(jnp.float32)
    o_ref[...] = total.astype(o_ref.dtype)


def axis_scatter(x, axis, number, dtype):
    size = lax.axis_size(axis)
    return pl.pallas_call(
        functools.partial(axis_scatter_kernel, axis, size),
        out_shape=jax.ShapeDtypeStruct(x.shape[1:], dtype),
        in_specs=[pl.BlockSpec(memory_space=pltpu.VMEM)],
        out_specs=pl.BlockSpec(memory_space=pltpu.VMEM),
        scratch_shapes=[
            pltpu.VMEM((size - 1,) + x.shape[1:], x.dtype),
            pltpu.SemaphoreType.DMA((size - 1,)),
            pltpu.SemaphoreType.DMA((size - 1,)),
        ],
        compiler_params=pltpu.CompilerParams(
            collective_id=number, has_side_effects=True, vmem_limit_bytes=VMEM_LIMIT
        ),
        name="axis_scatter_%d" % number,
    )(x)


def cube_places(axis, outer, rows):
    a = lax.axis_index(axis)
    context = lax.axis_index("context")
    x, c = context // 2, lax.rem(context, 2)
    outer_places = [wrap(a + k, outer) for k in range(outer)]
    row_places = [wrap(x + j, rows) for j in range(rows)]
    outer_peers = [{axis: place} for place in outer_places]
    row_peers = [{"context": place * 2 + c} for place in row_places]
    core_peer = {"context": x * 2 + (1 - c)}
    return a, x, c, outer_places, row_places, outer_peers, row_peers, core_peer


def cube_gather_kernel(axis, outer, rows, x_ref, o_ref, s1, r1, s2, r2, s3, r3, own_sem):
    a, x, c, outer_places, row_places, outer_peers, row_peers, core_peer = cube_places(
        axis, outer, rows
    )
    greet(outer_peers[1:] + row_peers[1:] + [core_peer])
    own = pltpu.make_async_copy(x_ref, o_ref.at[a, x, c], own_sem)
    own.start()
    sent = []
    first = [None] * outer
    for k in range(1, outer):
        first[k] = send(x_ref, o_ref.at[a, x, c], s1.at[k], r1.at[k], outer_peers[k])
    second = {}
    third = {}
    own.wait()
    for k in range(outer):
        if k:
            first[k].wait_recv()
        held = o_ref.at[wrap(a - k, outer), x, c]
        for j in range(1, rows):
            second[k, j] = send(held, held, s2.at[k, j], r2.at[k, j], row_peers[j])
        third[k, 0] = send(held, held, s3.at[k, 0], r3.at[k, 0], core_peer)
    for k in range(outer):
        for j in range(1, rows):
            second[k, j].wait_recv()
            held = o_ref.at[wrap(a - k, outer), wrap(x - j, rows), c]
            third[k, j] = send(held, held, s3.at[k, j], r3.at[k, j], core_peer)
    for copy in third.values():
        copy.wait_recv()
    for copy in first[1:] + list(second.values()) + list(third.values()):
        copy.wait_send()


def cube_gather(x, axis, number):
    outer, rows = lax.axis_size(axis), lax.axis_size("context") // 2
    pair = pltpu.SemaphoreType.DMA((outer, rows))
    return pl.pallas_call(
        functools.partial(cube_gather_kernel, axis, outer, rows),
        out_shape=jax.ShapeDtypeStruct((outer, rows, 2) + x.shape, x.dtype),
        in_specs=[pl.BlockSpec(memory_space=pltpu.VMEM)],
        out_specs=pl.BlockSpec(memory_space=pltpu.VMEM),
        scratch_shapes=[
            pltpu.SemaphoreType.DMA((outer,)),
            pltpu.SemaphoreType.DMA((outer,)),
            pair,
            pair,
            pair,
            pair,
            pltpu.SemaphoreType.DMA,
        ],
        compiler_params=pltpu.CompilerParams(
            collective_id=number, has_side_effects=True, vmem_limit_bytes=VMEM_LIMIT
        ),
        name="cube_gather_%d" % number,
    )(x)


def cube_scatter_kernel(
    axis, outer, rows, x_ref, o_ref, h1, part, h2, share, h3, s1, r1, s2, r2, s3, r3
):
    a, x, c, outer_places, row_places, outer_peers, row_peers, core_peer = cube_places(
        axis, outer, rows
    )
    greet(outer_peers[1:] + row_peers[1:] + [core_peer])
    order = [(k, j) for j in reversed(range(rows)) for k in reversed(range(outer))]
    first = {}
    for k, j in order:
        first[k, j] = send(
            x_ref.at[outer_places[k], row_places[j], 1 - c],
            h1.at[outer_places[k], row_places[j]],
            s1.at[k, j],
            r1.at[k, j],
            core_peer,
        )
    second = {}
    for k, j in order:
        first[k, j].wait_recv()
        total = x_ref[outer_places[k], row_places[j], c].astype(jnp.float32) + h1[
            outer_places[k], row_places[j]
        ].astype(jnp.float32)
        part[k, j] = total.astype(part.dtype)
        if j:
            second[k, j] = send(
                part.at[k, j], h2.at[k, j], s2.at[k, j], r2.at[k, j], row_peers[j]
            )
    third = {}
    for k in reversed(range(outer)):
        total = part[k, 0].astype(jnp.float32)
        for j in range(1, rows):
            second[k, j].wait_recv()
            total = total + h2[k, j].astype(jnp.float32)
        if k:
            share[k] = total.astype(share.dtype)
            third[k] = send(share.at[k], h3.at[k], s3.at[k], r3.at[k], outer_peers[k])
    for k in range(1, outer):
        third[k].wait_recv()
        total = total + h3[k].astype(jnp.float32)
    o_ref[...] = total
    for copy in list(first.values()) + list(second.values()) + list(third.values()):
        copy.wait_send()


def cube_scatter(x, axis, number):
    outer, rows = lax.axis_size(axis), lax.axis_size("context") // 2
    block = x.shape[3:]
    pair = pltpu.SemaphoreType.DMA((outer, rows))
    return pl.pallas_call(
        functools.partial(cube_scatter_kernel, axis, outer, rows),
        out_shape=jax.ShapeDtypeStruct(block, jnp.float32),
        in_specs=[pl.BlockSpec(memory_space=pltpu.VMEM)],
        out_specs=pl.BlockSpec(memory_space=pltpu.VMEM),
        scratch_shapes=[
            pltpu.VMEM((outer, rows) + block, x.dtype),
            pltpu.VMEM((outer, rows) + block, x.dtype),
            pltpu.VMEM((outer, rows) + block, x.dtype),
            pltpu.VMEM((outer,) + block, x.dtype),
            pltpu.VMEM((outer,) + block, x.dtype),
            pair,
            pair,
            pair,
            pair,
            pltpu.SemaphoreType.DMA((outer,)),
            pltpu.SemaphoreType.DMA((outer,)),
        ],
        compiler_params=pltpu.CompilerParams(
            collective_id=number, has_side_effects=True, vmem_limit_bytes=VMEM_LIMIT
        ),
        name="cube_scatter_%d" % number,
    )(x)


def norm_scale(values):
    return lax.rsqrt(jnp.mean(values * values, axis=-1, keepdims=True) + norm_eps)


def rope_tables(positions):
    half_dim = HEAD_FEATURES // 2
    frequency = rope_base ** (-(2.0 * jnp.arange(half_dim, dtype=jnp.float32)) / HEAD_FEATURES)
    angles = positions.astype(jnp.float32)[:, None] * frequency[None, :]
    return (jnp.cos(angles), jnp.sin(angles))


def rotate(vectors, cos_table, sin_table):
    half_dim = HEAD_FEATURES // 2
    a, b = vectors[..., :half_dim], vectors[..., half_dim:]
    cos_wide, sin_wide = cos_table[:, None, :], sin_table[:, None, :]
    return jnp.concatenate([a * cos_wide - b * sin_wide, b * cos_wide + a * sin_wide], axis=-1)


def unrotate(vectors, cos_table, sin_table):
    return rotate(vectors, cos_table, -sin_table)


def wide_dot(a, b):
    return jnp.dot(a, b, preferred_element_type=jnp.float32)


def dot_last(a, b):
    return lax.dot_general(a, b, (((1,), (1,)), ((), ())), preferred_element_type=jnp.float32)


def dot_first(a, b):
    return lax.dot_general(a, b, (((0,), (0,)), ((), ())), preferred_element_type=jnp.float32)


def pad_lanes(parts, rows):
    joined = jnp.concatenate(parts, axis=1)
    missing = -joined.shape[1] % 128
    return jnp.concatenate([joined, jnp.zeros((rows, missing), joined.dtype)], axis=1)


def high_low(values):
    high = values.astype(jnp.bfloat16)
    return [high, (values - high.astype(jnp.float32)).astype(jnp.bfloat16)]


def on_device(
    hidden_in,
    segments,
    routes,
    attn_gain,
    w_query,
    key_projection,
    value_projection,
    w_out,
    moe_gain,
    w_router,
    w_gate,
    w_up,
    w_down,
    out_grad,
):
    seq_rows = hidden_in.shape[1]
    model_width = hidden_in.shape[2]
    quarter = routes.shape[1]
    expert_count = w_router.shape[1]
    tensor_rank = lax.axis_index("tensor")
    context_rank = lax.axis_index("context")
    fsdp_size, context_size, tensor_size = (
        lax.axis_size("fsdp"),
        lax.axis_size("context"),
        lax.axis_size("tensor"),
    )
    row_count = context_size // 2
    quarter_first = tensor_rank * quarter
    owned = w_query.shape[0]
    q_width, kv_width = w_query.shape[1], key_projection.shape[1]
    out_width = w_out.shape[0]
    seg_columns = seq_rows // owned
    low_segs = segments[0].astype(jnp.bfloat16)
    packed = pad_lanes(
        [
            w_query,
            key_projection,
            value_projection,
            w_out.T,
            w_router,
            attn_gain[:, None],
            moe_gain[:, None],
            low_segs.reshape(seg_columns, owned).T,
        ],
        owned,
    )
    gathered = cube_gather(packed, "fsdp", 1)
    all_small = gathered[..., q_width + 2 * kv_width + out_width :]
    gathered = gathered.reshape(model_width, packed.shape[1])
    qkv_width = q_width + 2 * kv_width
    qkv_w = gathered[:, :qkv_width]
    out_wt = gathered[:, qkv_width : qkv_width + out_width]
    small = gathered[:, qkv_width + out_width :]
    router_w = small[:, :expert_count]
    gain_one = small[:, expert_count].astype(jnp.float32)
    gain_two = small[:, expert_count + 1].astype(jnp.float32)
    fsdp_rank = lax.axis_index("fsdp")
    seq_small = lax.dynamic_index_in_dim(all_small, fsdp_rank, 0, keepdims=False)
    all_segs = (
        seq_small[..., expert_count + 2 : expert_count + 2 + seg_columns]
        .transpose(0, 1, 3, 2)
        .reshape(context_size * seq_rows)
        .astype(jnp.float32)
    )
    gate_full = lax.all_gather(w_gate[0], "fsdp", axis=0, tiled=True)
    up_full = lax.all_gather(w_up[0], "fsdp", axis=0, tiled=True)
    down_full = lax.all_gather(w_down[0], "fsdp", axis=1, tiled=True)
    all_out_grad = cube_gather(out_grad[0], "tensor", 2).reshape(-1, model_width)

    hidden = hidden_in[0].astype(jnp.float32)
    scale_one = norm_scale(hidden)
    unit_one = hidden * scale_one
    normed_input = (unit_one * gain_one).astype(jnp.bfloat16)
    positions = context_rank * seq_rows + jnp.arange(seq_rows, dtype=jnp.int32)
    cos_table, sin_table = rope_tables(positions)
    query_heads = q_width // HEAD_FEATURES
    kv_heads = kv_width // HEAD_FEATURES
    group_size = query_heads // kv_heads
    projected = wide_dot(normed_input, qkv_w)
    queries = (
        rotate(
            projected[:, :q_width].reshape(seq_rows, query_heads, HEAD_FEATURES),
            cos_table,
            sin_table,
        )
        * HEAD_FEATURES ** (-0.5)
    ).astype(jnp.bfloat16)
    grouped_queries = queries.reshape(seq_rows, kv_heads, group_size, HEAD_FEATURES)
    keys = (
        rotate(
            projected[:, q_width : q_width + kv_width].reshape(seq_rows, kv_heads, HEAD_FEATURES),
            cos_table,
            sin_table,
        )
        .astype(jnp.bfloat16)
        .reshape(seq_rows, kv_width)
    )
    values = projected[:, q_width + kv_width :].astype(jnp.bfloat16)
    all_kv = axis_gather(jnp.concatenate([keys, values], axis=1), "context", 3)
    total_keys = context_size * seq_rows
    all_kv = all_kv.reshape(total_keys, 2, kv_heads, HEAD_FEATURES)
    all_keys, all_values = all_kv[:, 0], all_kv[:, 1]
    own_seg = segments[0].astype(jnp.float32)
    key_pos = jnp.arange(total_keys, dtype=jnp.int32)
    allowed = (key_pos[None, :] <= positions[:, None]) & (all_segs[None, :] == own_seg[:, None])
    scores = jnp.einsum(
        "rkgd,lkd->kgrl", grouped_queries, all_keys, preferred_element_type=jnp.float32
    )
    scores = jnp.where(allowed, scores, -jnp.inf)
    raised_scores = jnp.exp(scores - jnp.max(scores, axis=-1, keepdims=True))
    probs = raised_scores / jnp.sum(raised_scores, axis=-1, keepdims=True)
    probs_low = probs.astype(jnp.bfloat16)
    mixed = (
        jnp.einsum("kgrl,lkd->rkgd", probs_low, all_values, preferred_element_type=jnp.float32)
        .astype(jnp.bfloat16)
        .reshape(seq_rows, q_width)
    )
    attn_part = dot_last(mixed, out_wt).astype(jnp.bfloat16)
    attn_out = axis_scatter(
        attn_part.reshape(tensor_size, quarter, model_width), "tensor", 4, jnp.float32
    )
    res_rows = lax.dynamic_slice_in_dim(hidden, quarter_first, quarter, 0) + attn_out
    scale_two = norm_scale(res_rows)
    unit_two = res_rows * scale_two
    normed_two = (unit_two * gain_two).astype(jnp.bfloat16)
    logits = wide_dot(normed_two, router_w)
    named = jnp.any(
        routes[0][:, :, None] == jnp.arange(expert_count, dtype=jnp.int32)[None, None, :], axis=1
    )
    top_logit = jnp.max(jnp.where(named, logits, -jnp.inf), axis=-1, keepdims=True)
    raised = jnp.where(named, jnp.exp(jnp.where(named, logits - top_logit, 0.0)), 0.0)
    gate_weight = raised / jnp.sum(raised, axis=-1, keepdims=True)
    sent = pad_lanes([normed_two] + high_low(gate_weight), quarter)
    arrived = cube_gather(sent, "tensor", 5).reshape(-1, sent.shape[1])
    token_rows = arrived[:, :model_width]
    arrived_gates = arrived[:, model_width : model_width + expert_count].astype(
        jnp.float32
    ) + arrived[:, model_width + expert_count : model_width + 2 * expert_count].astype(jnp.float32)
    own_expert = (
        jnp.arange(expert_count, dtype=jnp.int32) == context_rank * tensor_size + tensor_rank
    )
    own_gate = jnp.sum(jnp.where(own_expert, arrived_gates, 0.0), axis=-1, keepdims=True)
    gate_pre = wide_dot(token_rows, gate_full)
    up_pre = wide_dot(token_rows, up_full)
    gate_sig = jax.nn.sigmoid(gate_pre)
    activated = (gate_pre * gate_sig * up_pre).astype(jnp.bfloat16)
    expert_out = wide_dot(activated, down_full).astype(jnp.bfloat16).astype(jnp.float32)
    wide_grads = all_out_grad.astype(jnp.float32)
    out_grads = (own_gate * wide_grads).astype(jnp.bfloat16)
    own_picks = jnp.sum(wide_grads * expert_out, axis=-1, keepdims=True)
    pick_table = jnp.where(own_expert, own_picks, 0.0)
    act_grads = dot_last(out_grads, down_full)
    gate_grads = (act_grads * up_pre * gate_sig * (1.0 + gate_pre * (1.0 - gate_sig))).astype(
        jnp.bfloat16
    )
    up_grads = (act_grads * gate_pre * gate_sig).astype(jnp.bfloat16)
    row_grads = (dot_last(gate_grads, gate_full) + dot_last(up_grads, up_full)).astype(jnp.bfloat16)
    token_count = row_grads.shape[0]
    returned = pad_lanes(
        [row_grads, (own_gate * expert_out).astype(jnp.bfloat16)] + high_low(pick_table),
        token_count,
    )
    summed = cube_scatter(
        returned.reshape(tensor_size, row_count, 2, quarter, returned.shape[1]), "tensor", 6
    )
    block_output = (res_rows + summed[:, model_width : 2 * model_width]).astype(jnp.bfloat16)[None]
    picks = (
        summed[:, 2 * model_width : 2 * model_width + expert_count]
        + summed[:, 2 * model_width + expert_count : 2 * model_width + 2 * expert_count]
    )
    logit_grads = (
        gate_weight * (picks - jnp.sum(gate_weight * picks, axis=-1, keepdims=True))
    ).astype(jnp.bfloat16)
    router_part = dot_first(normed_two, logit_grads)
    norm_two_grads = summed[:, :model_width] + dot_last(logit_grads, router_w)

    expert_terms = jnp.concatenate(
        [
            dot_first(token_rows, gate_grads).astype(jnp.bfloat16),
            dot_first(token_rows, up_grads).astype(jnp.bfloat16),
            dot_first(out_grads, activated).astype(jnp.bfloat16),
        ],
        axis=1,
    )
    expert_grads = lax.psum_scatter(expert_terms, "fsdp", scatter_dimension=0, tiled=True).astype(
        jnp.float32
    )
    hidden_units = w_gate.shape[2]
    gate_grad = expert_grads[None, :, :hidden_units]
    up_grad = expert_grads[None, :, hidden_units : 2 * hidden_units]
    down_grad = expert_grads[:, 2 * hidden_units :].T[None]

    grad_rows = out_grad[0].astype(jnp.float32)
    scaled_grads = norm_two_grads * gain_two
    gain_two_part = jnp.sum(norm_two_grads * unit_two, axis=0)
    res_grads = grad_rows + scale_two * (
        scaled_grads - unit_two * jnp.mean(scaled_grads * unit_two, axis=-1, keepdims=True)
    )
    attn_grads = axis_gather(res_grads.astype(jnp.bfloat16), "tensor", 7).reshape(
        seq_rows, model_width
    )
    out_term = dot_first(attn_grads, mixed)
    mixed_grads = (
        wide_dot(attn_grads, out_wt)
        .astype(jnp.bfloat16)
        .reshape(seq_rows, kv_heads, group_size, HEAD_FEATURES)
    )
    prob_grads = jnp.einsum(
        "rkgd,lkd->kgrl", mixed_grads, all_values, preferred_element_type=jnp.float32
    )
    delta = jnp.sum(probs * prob_grads, axis=-1, keepdims=True)
    score_grads = (probs * (prob_grads - delta)).astype(jnp.bfloat16)
    query_sums = jnp.einsum(
        "kgrl,lkd->rkgd", score_grads, all_keys, preferred_element_type=jnp.float32
    )
    key_terms = jnp.einsum(
        "kgrl,rkgd->lkd", score_grads, grouped_queries, preferred_element_type=jnp.float32
    )
    value_terms = jnp.einsum(
        "kgrl,rkgd->lkd", probs_low, mixed_grads, preferred_element_type=jnp.float32
    )
    kv_terms = jnp.concatenate(
        [key_terms.reshape(total_keys, kv_width), value_terms.reshape(total_keys, kv_width)], axis=1
    ).astype(jnp.bfloat16)
    kv_sums = axis_scatter(
        kv_terms.reshape(context_size, seq_rows, 2 * kv_width), "context", 8, jnp.float32
    )
    key_grads = unrotate(
        kv_sums[:, :kv_width].reshape(seq_rows, kv_heads, HEAD_FEATURES), cos_table, sin_table
    ).reshape(seq_rows, kv_width)
    query_grads = unrotate(
        query_sums.reshape(seq_rows, query_heads, HEAD_FEATURES) * HEAD_FEATURES ** (-0.5),
        cos_table,
        sin_table,
    ).reshape(seq_rows, q_width)
    qkv_grads = jnp.concatenate([query_grads, key_grads, kv_sums[:, kv_width:]], axis=1).astype(
        jnp.bfloat16
    )
    normed_part = dot_last(qkv_grads, qkv_w).astype(jnp.bfloat16)
    qkv_term = dot_first(normed_input, qkv_grads)
    normed_grads = axis_scatter(
        normed_part.reshape(tensor_size, quarter, model_width), "tensor", 9, jnp.float32
    )
    own_unit = lax.dynamic_slice_in_dim(unit_one, quarter_first, quarter, 0)
    own_scale = lax.dynamic_slice_in_dim(scale_one, quarter_first, quarter, 0)
    scaled_one = normed_grads * gain_one
    gain_one_part = jnp.sum(normed_grads * own_unit, axis=0)
    input_grad = (
        res_grads
        + own_scale
        * (scaled_one - own_unit * jnp.mean(scaled_one * own_unit, axis=-1, keepdims=True))
    )[None]
    terms = pad_lanes(
        [qkv_term, out_term, router_part, gain_one_part[:, None], gain_two_part[:, None]],
        model_width,
    ).astype(jnp.bfloat16)
    sums = cube_scatter(
        terms.reshape(fsdp_size, row_count, 2, owned, terms.shape[1]), "fsdp", 10
    )
    tail = sums[:, qkv_width + out_width :]
    shared = jnp.sum(
        axis_gather(tail.astype(jnp.bfloat16), "tensor", 11).astype(jnp.float32), axis=0
    )
    return (
        block_output,
        input_grad,
        shared[:, expert_count],
        sums[:, :q_width],
        sums[:, q_width : q_width + kv_width],
        sums[:, q_width + kv_width : qkv_width],
        sums[:, qkv_width : qkv_width + out_width].T,
        shared[:, expert_count + 1],
        shared[:, :expert_count],
        gate_grad,
        up_grad,
        down_grad,
    )


def solution(mesh):
    return jax.shard_map(
        on_device,
        mesh=mesh,
        in_specs=(
            P("fsdp", "context", None),
            P("fsdp", "context"),
            P("fsdp", ("context", "tensor"), None),
            P(("fsdp", "context")),
            P(("fsdp", "context"), "tensor"),
            P(("fsdp", "context"), "tensor"),
            P(("fsdp", "context"), "tensor"),
            P("tensor", ("fsdp", "context")),
            P(("fsdp", "context")),
            P(("fsdp", "context"), None),
            P(("context", "tensor"), "fsdp", None),
            P(("context", "tensor"), "fsdp", None),
            P(("context", "tensor"), None, "fsdp"),
            P("fsdp", ("context", "tensor"), None),
        ),
        out_specs=(
            P("fsdp", ("context", "tensor"), None),
            P("fsdp", ("context", "tensor"), None),
            P(("fsdp", "context")),
            P(("fsdp", "context"), "tensor"),
            P(("fsdp", "context"), "tensor"),
            P(("fsdp", "context"), "tensor"),
            P("tensor", ("fsdp", "context")),
            P(("fsdp", "context")),
            P(("fsdp", "context"), None),
            P(("context", "tensor"), "fsdp", None),
            P(("context", "tensor"), "fsdp", None),
            P(("context", "tensor"), None, "fsdp"),
        ),
        check_vma=False,
    )
```

```python
import functools

import jax
import jax.numpy as jnp
from jax import lax
from jax.experimental import pallas as pl
from jax.experimental.pallas import tpu as pltpu
from jax.sharding import PartitionSpec as P

HEAD_FEATURES = 64
rope_base = 10000.0
norm_eps = 1e-06
MESH = pl.DeviceIdType.MESH
VMEM_LIMIT = 48 * 1024 * 1024


def wrap(value, size):
    return lax.rem(value + size, size)


def greet(devices):
    barrier = pltpu.get_barrier_semaphore()
    for device in devices:
        pl.semaphore_signal(barrier, inc=1, device_id=device, device_id_type=MESH)
    pl.semaphore_wait(barrier, len(devices))


def send(source, target, send_sem, recv_sem, device):
    copy = pltpu.make_async_remote_copy(
        src_ref=source,
        dst_ref=target,
        send_sem=send_sem,
        recv_sem=recv_sem,
        device_id=device,
        device_id_type=MESH,
    )
    copy.start()
    return copy


def axis_gather_kernel(axis, size, x_ref, o_ref, send_sem, recv_sem, own_sem):
    me = lax.axis_index(axis)
    peers = [{axis: wrap(me + k, size)} for k in range(1, size)]
    greet(peers)
    copies = [
        send(x_ref, o_ref.at[me], send_sem.at[k], recv_sem.at[k], peers[k]) for k in range(size - 1)
    ]
    own = pltpu.make_async_copy(x_ref, o_ref.at[me], own_sem)
    own.start()
    own.wait()
    for copy in copies:
        copy.wait()


def axis_gather(x, axis, number):
    size = lax.axis_size(axis)
    return pl.pallas_call(
        functools.partial(axis_gather_kernel, axis, size),
        out_shape=jax.ShapeDtypeStruct((size,) + x.shape, x.dtype),
        in_specs=[pl.BlockSpec(memory_space=pltpu.VMEM)],
        out_specs=pl.BlockSpec(memory_space=pltpu.VMEM),
        scratch_shapes=[
            pltpu.SemaphoreType.DMA((size - 1,)),
            pltpu.SemaphoreType.DMA((size - 1,)),
            pltpu.SemaphoreType.DMA,
        ],
        compiler_params=pltpu.CompilerParams(
            collective_id=number, has_side_effects=True, vmem_limit_bytes=VMEM_LIMIT
        ),
        name="axis_gather_%d" % number,
    )(x)


def axis_scatter_kernel(axis, size, x_ref, o_ref, held, send_sem, recv_sem):
    me = lax.axis_index(axis)
    places = [wrap(me + k, size) for k in range(1, size)]
    greet([{axis: place} for place in places])
    copies = [
        send(x_ref.at[places[k]], held.at[k], send_sem.at[k], recv_sem.at[k], {axis: places[k]})
        for k in range(size - 1)
    ]
    for copy in copies:
        copy.wait()
    total = x_ref[me].astype(jnp.float32)
    for k in range(size - 1):
        total = total + held[k].astype(jnp.float32)
    o_ref[...] = total.astype(o_ref.dtype)


def axis_scatter(x, axis, number, dtype):
    size = lax.axis_size(axis)
    return pl.pallas_call(
        functools.partial(axis_scatter_kernel, axis, size),
        out_shape=jax.ShapeDtypeStruct(x.shape[1:], dtype),
        in_specs=[pl.BlockSpec(memory_space=pltpu.VMEM)],
        out_specs=pl.BlockSpec(memory_space=pltpu.VMEM),
        scratch_shapes=[
            pltpu.VMEM((size - 1,) + x.shape[1:], x.dtype),
            pltpu.SemaphoreType.DMA((size - 1,)),
            pltpu.SemaphoreType.DMA((size - 1,)),
        ],
        compiler_params=pltpu.CompilerParams(
            collective_id=number, has_side_effects=True, vmem_limit_bytes=VMEM_LIMIT
        ),
        name="axis_scatter_%d" % number,
    )(x)


def cube_places(axis, outer, rows):
    a = lax.axis_index(axis)
    context = lax.axis_index("context")
    x, c = context // 2, lax.rem(context, 2)
    outer_places = [wrap(a + k, outer) for k in range(outer)]
    row_places = [wrap(x + j, rows) for j in range(rows)]
    outer_peers = [{axis: place} for place in outer_places]
    row_peers = [{"context": place * 2 + c} for place in row_places]
    core_peer = {"context": x * 2 + (1 - c)}
    return a, x, c, outer_places, row_places, outer_peers, row_peers, core_peer


def cube_gather_kernel(axis, outer, rows, pieces, beside, *refs):
    if beside:
        x_ref, y_ref, o_ref, z_ref, s1, r1, s2, r2, s3, r3, own_sem, s4, r4, own_y = refs
    else:
        x_ref, o_ref, s1, r1, s2, r2, s3, r3, own_sem = refs
    a, x, c, outer_places, row_places, outer_peers, row_peers, core_peer = cube_places(
        axis, outer, rows
    )
    side_peers = []
    if beside:
        me = lax.axis_index("tensor")
        side_peers = [{"tensor": wrap(me + k, beside)} for k in range(1, beside)]
    greet(outer_peers[1:] + row_peers[1:] + [core_peer] + side_peers)
    own = pltpu.make_async_copy(x_ref, o_ref.at[a, x, c], own_sem)
    own.start()
    height = x_ref.shape[0] // pieces
    spans = [pl.ds(p * height, height) for p in range(pieces)]
    first, second, third, side = {}, {}, {}, []
    for p in range(pieces):
        for k in range(1, outer):
            first[p, k] = send(
                x_ref.at[spans[p]],
                o_ref.at[a, x, c, spans[p]],
                s1.at[p, k],
                r1.at[p, k],
                outer_peers[k],
            )
    if beside:
        own_side = pltpu.make_async_copy(y_ref, z_ref.at[me], own_y)
        own_side.start()
        side = [
            send(y_ref, z_ref.at[me], s4.at[k], r4.at[k], side_peers[k]) for k in range(beside - 1)
        ]
    own.wait()
    blocks = [(p, 0) for p in range(pieces)]
    blocks += [(p, k) for p in range(pieces) for k in range(1, outer)]
    for p, k in blocks:
        if k:
            first[p, k].wait_recv()
        held = o_ref.at[wrap(a - k, outer), x, c, spans[p]]
        for j in range(1, rows):
            second[p, k, j] = send(held, held, s2.at[p, k, j], r2.at[p, k, j], row_peers[j])
        third[p, k, 0] = send(held, held, s3.at[p, k, 0], r3.at[p, k, 0], core_peer)
    for p, k in blocks:
        for j in range(1, rows):
            second[p, k, j].wait_recv()
            held = o_ref.at[wrap(a - k, outer), wrap(x - j, rows), c, spans[p]]
            third[p, k, j] = send(held, held, s3.at[p, k, j], r3.at[p, k, j], core_peer)
    for copy in third.values():
        copy.wait_recv()
    for copy in list(first.values()) + list(second.values()) + list(third.values()):
        copy.wait_send()
    if beside:
        own_side.wait()
    for copy in side:
        copy.wait()


def cube_gather(x, axis, number, beside=None):
    outer, rows = lax.axis_size(axis), lax.axis_size("context") // 2
    pieces = 2 if x.shape[0] % 32 == 0 else 1
    single = pltpu.SemaphoreType.DMA((pieces, outer))
    pair = pltpu.SemaphoreType.DMA((pieces, outer, rows))
    vmem = pl.BlockSpec(memory_space=pltpu.VMEM)
    shapes = [jax.ShapeDtypeStruct((outer, rows, 2) + x.shape, x.dtype)]
    scratch = [single, single, pair, pair, pair, pair, pltpu.SemaphoreType.DMA]
    args = [x]
    side = 0
    if beside is not None:
        side = lax.axis_size("tensor")
        args.append(beside)
        shapes.append(jax.ShapeDtypeStruct((side,) + beside.shape, beside.dtype))
        several = pltpu.SemaphoreType.DMA((side - 1,))
        scratch += [several, several, pltpu.SemaphoreType.DMA]
    outs = pl.pallas_call(
        functools.partial(cube_gather_kernel, axis, outer, rows, pieces, side),
        out_shape=shapes,
        in_specs=[vmem] * len(args),
        out_specs=[vmem] * len(shapes),
        scratch_shapes=scratch,
        compiler_params=pltpu.CompilerParams(
            collective_id=number, has_side_effects=True, vmem_limit_bytes=VMEM_LIMIT
        ),
        name="cube_gather_%d" % number,
    )(*args)
    return outs if beside is not None else outs[0]


def scatter_and_spread_kernel(
    size, rows, x_ref, y_ref, o_ref, z_ref, held, s1, r1, s2, r2, s3, r3, own_sem
):
    a, x, c, places, row_places, peers, row_peers, core_peer = cube_places("tensor", size, rows)
    greet(peers[1:] + row_peers[1:] + [core_peer])
    first = [
        send(x_ref.at[places[k]], held.at[k - 1], s1.at[k], r1.at[k], peers[k])
        for k in range(1, size)
    ]
    own = [
        pltpu.make_async_copy(y_ref.at[k], z_ref.at[k, x, c], own_sem.at[k]) for k in range(size)
    ]
    for copy in own:
        copy.start()
    second, third = {}, {}
    for k in range(size):
        for j in range(1, rows):
            second[k, j] = send(
                y_ref.at[k], z_ref.at[k, x, c], s2.at[k, j], r2.at[k, j], row_peers[j]
            )
        third[k, 0] = send(y_ref.at[k], z_ref.at[k, x, c], s3.at[k, 0], r3.at[k, 0], core_peer)
    for k in range(size):
        for j in range(1, rows):
            second[k, j].wait_recv()
            block = z_ref.at[k, wrap(x - j, rows), c]
            third[k, j] = send(block, block, s3.at[k, j], r3.at[k, j], core_peer)
    for copy in first:
        copy.wait()
    total = x_ref[a].astype(jnp.float32)
    for k in range(size - 1):
        total = total + held[k].astype(jnp.float32)
    o_ref[...] = total
    for copy in own:
        copy.wait()
    for copy in second.values():
        copy.wait_send()
    for copy in third.values():
        copy.wait()


def scatter_and_spread(x, y, number):
    size, rows = lax.axis_size("tensor"), lax.axis_size("context") // 2
    vmem = pl.BlockSpec(memory_space=pltpu.VMEM)
    several = pltpu.SemaphoreType.DMA((size,))
    pair = pltpu.SemaphoreType.DMA((size, rows))
    return pl.pallas_call(
        functools.partial(scatter_and_spread_kernel, size, rows),
        out_shape=[
            jax.ShapeDtypeStruct(x.shape[1:], jnp.float32),
            jax.ShapeDtypeStruct((size, rows, 2) + y.shape[1:], y.dtype),
        ],
        in_specs=[vmem] * 2,
        out_specs=[vmem] * 2,
        scratch_shapes=[
            pltpu.VMEM((size - 1,) + x.shape[1:], x.dtype),
            several,
            several,
            pair,
            pair,
            pair,
            pair,
            several,
        ],
        compiler_params=pltpu.CompilerParams(
            collective_id=number, has_side_effects=True, vmem_limit_bytes=VMEM_LIMIT
        ),
        name="scatter_and_spread_%d" % number,
    )(x, y)


def gather_and_fold_kernel(
    size, rows, x_ref, y_ref, o_ref, z_ref, h1, part, h2, s1, r1, s2, r2, s3, r3, own_sem
):
    a, x, c, places, row_places, peers, row_peers, core_peer = cube_places("tensor", size, rows)
    greet(peers[1:] + row_peers[1:] + [core_peer])
    first = [
        send(x_ref, o_ref.at[a], s1.at[k], r1.at[k], peers[k]) for k in range(1, size)
    ]
    own = pltpu.make_async_copy(x_ref, o_ref.at[a], own_sem)
    own.start()
    order = [(k, j) for j in reversed(range(rows)) for k in range(size)]
    second, third = {}, {}
    for k, j in order:
        place = row_places[j]
        second[k, j] = send(
            y_ref.at[k, place, 1 - c], h1.at[k, place], s2.at[k, j], r2.at[k, j], core_peer
        )
    for k, j in order:
        place = row_places[j]
        second[k, j].wait_recv()
        total = y_ref[k, place, c].astype(jnp.float32) + h1[k, place].astype(jnp.float32)
        part[k, j] = total.astype(part.dtype)
        if j:
            third[k, j] = send(part.at[k, j], h2.at[k, j], s3.at[k, j], r3.at[k, j], row_peers[j])
    for k in range(size):
        total = part[k, 0].astype(jnp.float32)
        for j in range(1, rows):
            third[k, j].wait_recv()
            total = total + h2[k, j].astype(jnp.float32)
        z_ref[k] = total.astype(z_ref.dtype)
    own.wait()
    for copy in first:
        copy.wait()
    for copy in list(second.values()) + list(third.values()):
        copy.wait_send()


def gather_and_fold(x, y, number):
    size, rows = lax.axis_size("tensor"), lax.axis_size("context") // 2
    vmem = pl.BlockSpec(memory_space=pltpu.VMEM)
    several = pltpu.SemaphoreType.DMA((size,))
    pair = pltpu.SemaphoreType.DMA((size, rows))
    blocks = pltpu.VMEM((size, rows) + y.shape[3:], y.dtype)
    return pl.pallas_call(
        functools.partial(gather_and_fold_kernel, size, rows),
        out_shape=[
            jax.ShapeDtypeStruct((size,) + x.shape, x.dtype),
            jax.ShapeDtypeStruct((size,) + y.shape[3:], y.dtype),
        ],
        in_specs=[vmem] * 2,
        out_specs=[vmem] * 2,
        scratch_shapes=[
            blocks,
            blocks,
            blocks,
            several,
            several,
            pair,
            pair,
            pair,
            pair,
            pltpu.SemaphoreType.DMA,
        ],
        compiler_params=pltpu.CompilerParams(
            collective_id=number, has_side_effects=True, vmem_limit_bytes=VMEM_LIMIT
        ),
        name="gather_and_fold_%d" % number,
    )(x, y)


def expert_kernel(
    experts, chunk, e_ref, tok, grads, wg, wu, wd, rows_o, out_o, terms_o, acc_g, acc_u, acc_d
):
    own = e_ref[0]
    width = grads.shape[1]
    hidden_units = wg.shape[1]
    acc_g[...] = jnp.zeros_like(acc_g)
    acc_u[...] = jnp.zeros_like(acc_u)
    acc_d[...] = jnp.zeros_like(acc_d)
    lane = lax.broadcasted_iota(jnp.int32, (chunk, 128), 1)

    def step(i, carried):
        span = pl.ds(pl.multiple_of(i * chunk, chunk), chunk)
        rows = tok[span, :width]
        table = tok[span, width:].astype(jnp.float32)
        gate = jnp.sum(
            jnp.where((lane == own) | (lane == own + experts), table, 0.0), axis=1, keepdims=True
        )
        wide = grads[span, :].astype(jnp.float32)
        gate_pre = wide_dot(rows, wg[...])
        up_pre = wide_dot(rows, wu[...])
        sig = jax.nn.sigmoid(gate_pre)
        swish = gate_pre * sig
        activated = (swish * up_pre).astype(jnp.bfloat16)
        result = wide_dot(activated, wd[...]).astype(jnp.bfloat16).astype(jnp.float32)
        out_o[span, :] = (gate * result).astype(jnp.bfloat16)
        pick = jnp.sum(wide * result, axis=1, keepdims=True)
        out_grads = (gate * wide).astype(jnp.bfloat16)
        act_grads = dot_last(out_grads, wd[...])
        gate_grads = (act_grads * up_pre * sig * (1.0 + gate_pre * (1.0 - sig))).astype(
            jnp.bfloat16
        )
        up_grads = (act_grads * swish).astype(jnp.bfloat16)
        rows_o[span, :width] = (
            dot_last(gate_grads, wg[...]) + dot_last(up_grads, wu[...])
        ).astype(jnp.bfloat16)
        high = pick.astype(jnp.bfloat16).astype(jnp.float32)
        rows_o[span, width:] = jnp.where(
            lane == own, high, jnp.where(lane == own + experts, pick - high, 0.0)
        ).astype(jnp.bfloat16)
        acc_g[...] += dot_first(rows, gate_grads)
        acc_u[...] += dot_first(rows, up_grads)
        acc_d[...] += dot_first(out_grads, activated)
        return carried

    lax.fori_loop(0, tok.shape[0] // chunk, step, 0)
    terms_o[:, :hidden_units] = acc_g[...].astype(jnp.bfloat16)
    terms_o[:, hidden_units : 2 * hidden_units] = acc_u[...].astype(jnp.bfloat16)
    terms_o[:, 2 * hidden_units :] = acc_d[...].astype(jnp.bfloat16)


def expert_pass(own, tok, grads, wg, wu, wd, experts):
    count, width = grads.shape
    hidden_units = wg.shape[1]
    vmem = pl.BlockSpec(memory_space=pltpu.VMEM)
    return pl.pallas_call(
        functools.partial(expert_kernel, experts, min(256, count)),
        out_shape=[
            jax.ShapeDtypeStruct(tok.shape, jnp.bfloat16),
            jax.ShapeDtypeStruct(grads.shape, jnp.bfloat16),
            jax.ShapeDtypeStruct((width, 3 * hidden_units), jnp.bfloat16),
        ],
        in_specs=[pl.BlockSpec(memory_space=pltpu.SMEM)] + [vmem] * 5,
        out_specs=[vmem] * 3,
        scratch_shapes=[pltpu.VMEM((width, hidden_units), jnp.float32)] * 3,
        compiler_params=pltpu.CompilerParams(vmem_limit_bytes=VMEM_LIMIT),
        name="expert_pass",
    )(own, tok, grads, wg, wu, wd)


def cube_scatter_kernel(axis, outer, rows, pieces, beside, lanes, *refs):
    if beside:
        x_ref, y_ref, o_ref, z_ref = refs[:4]
        h1, part, h2, share, h3, s1, r1, s2, r2, s3, r3 = refs[4:15]
        h4, tail, h5, s4, r4, s5, r5 = refs[15:]
    else:
        x_ref, o_ref, h1, part, h2, share, h3, s1, r1, s2, r2, s3, r3 = refs
    a, x, c, outer_places, row_places, outer_peers, row_peers, core_peer = cube_places(
        axis, outer, rows
    )
    side_peers = []
    if beside:
        me = lax.axis_index("tensor")
        side_places = [wrap(me + k, beside) for k in range(1, beside)]
        side_peers = [{"tensor": place} for place in side_places]
    greet(outer_peers[1:] + row_peers[1:] + [core_peer] + side_peers)
    height = x_ref.shape[3] // pieces
    spans = [pl.ds(p * height, height) for p in range(pieces)]
    order = [
        (p, k, j)
        for p in range(pieces)
        for j in reversed(range(rows))
        for k in reversed(range(outer))
    ]
    first, second, third, side, ends = {}, {}, {}, [], []
    for p, k, j in order:
        first[p, k, j] = send(
            x_ref.at[outer_places[k], row_places[j], 1 - c, spans[p]],
            h1.at[outer_places[k], row_places[j], spans[p]],
            s1.at[p, k, j],
            r1.at[p, k, j],
            core_peer,
        )
    if beside:
        side = [
            send(y_ref.at[side_places[k]], h4.at[k], s4.at[k], r4.at[k], side_peers[k])
            for k in range(beside - 1)
        ]
    for p in range(pieces):
        for j in reversed(range(rows)):
            for k in reversed(range(outer)):
                first[p, k, j].wait_recv()
                block = x_ref[outer_places[k], row_places[j], c, spans[p]].astype(jnp.float32)
                block = block + h1[outer_places[k], row_places[j], spans[p]].astype(jnp.float32)
                part[k, j, spans[p]] = block.astype(part.dtype)
                if j:
                    second[p, k, j] = send(
                        part.at[k, j, spans[p]],
                        h2.at[k, j, spans[p]],
                        s2.at[p, k, j],
                        r2.at[p, k, j],
                        row_peers[j],
                    )
    for p in range(pieces):
        for k in reversed(range(outer)):
            total = part[k, 0, spans[p]].astype(jnp.float32)
            for j in range(1, rows):
                second[p, k, j].wait_recv()
                total = total + h2[k, j, spans[p]].astype(jnp.float32)
            if k:
                share[k, spans[p]] = total.astype(share.dtype)
                third[p, k] = send(
                    share.at[k, spans[p]],
                    h3.at[k, spans[p]],
                    s3.at[p, k],
                    r3.at[p, k],
                    outer_peers[k],
                )
            else:
                o_ref[spans[p]] = total
    for p in range(pieces):
        total = o_ref[spans[p]]
        for k in range(1, outer):
            third[p, k].wait_recv()
            total = total + h3[k, spans[p]].astype(jnp.float32)
        o_ref[spans[p]] = total
    if beside:
        tail[...] = o_ref[:, lanes:].astype(tail.dtype)
        ends = [
            send(tail, h5.at[k], s5.at[k], r5.at[k], side_peers[k]) for k in range(beside - 1)
        ]
        for copy in side:
            copy.wait()
        total = y_ref[me].astype(jnp.float32)
        for k in range(beside - 1):
            total = total + h4[k].astype(jnp.float32)
        z_ref[...] = total
        for copy in ends:
            copy.wait()
        total = o_ref[:, lanes:]
        for k in range(beside - 1):
            total = total + h5[k].astype(jnp.float32)
        o_ref[:, lanes:] = total
    for copy in list(first.values()) + list(second.values()) + list(third.values()):
        copy.wait_send()


def cube_scatter(x, axis, number, beside=None, lanes=0):
    outer, rows = lax.axis_size(axis), lax.axis_size("context") // 2
    block = x.shape[3:]
    pieces = 2 if block[0] % 32 == 0 else 1
    single = pltpu.SemaphoreType.DMA((pieces, outer))
    pair = pltpu.SemaphoreType.DMA((pieces, outer, rows))
    vmem = pl.BlockSpec(memory_space=pltpu.VMEM)
    args = [x]
    shapes = [jax.ShapeDtypeStruct(block, jnp.float32)]
    scratch = [pltpu.VMEM((outer, rows) + block, x.dtype)] * 3
    scratch += [pltpu.VMEM((outer,) + block, x.dtype)] * 2
    scratch += [pair, pair, pair, pair, single, single]
    side = 0
    if beside is not None:
        side = lax.axis_size("tensor")
        args.append(beside)
        shapes.append(jax.ShapeDtypeStruct(beside.shape[1:], jnp.float32))
        several = pltpu.SemaphoreType.DMA((side - 1,))
        tail = (block[0], block[1] - lanes)
        scratch += [
            pltpu.VMEM((side - 1,) + beside.shape[1:], beside.dtype),
            pltpu.VMEM(tail, x.dtype),
            pltpu.VMEM((side - 1,) + tail, x.dtype),
            several,
            several,
            several,
            several,
        ]
    outs = pl.pallas_call(
        functools.partial(cube_scatter_kernel, axis, outer, rows, pieces, side, lanes),
        out_shape=shapes,
        in_specs=[vmem] * len(args),
        out_specs=[vmem] * len(shapes),
        scratch_shapes=scratch,
        compiler_params=pltpu.CompilerParams(
            collective_id=number, has_side_effects=True, vmem_limit_bytes=VMEM_LIMIT
        ),
        name="cube_scatter_%d" % number,
    )(*args)
    return outs if beside is not None else outs[0]


def norm_scale(values):
    return lax.rsqrt(jnp.mean(values * values, axis=-1, keepdims=True) + norm_eps)


def rope_tables(positions):
    half_dim = HEAD_FEATURES // 2
    frequency = rope_base ** (-(2.0 * jnp.arange(half_dim, dtype=jnp.float32)) / HEAD_FEATURES)
    angles = positions.astype(jnp.float32)[:, None] * frequency[None, :]
    return (jnp.cos(angles), jnp.sin(angles))


def rotate(vectors, cos_table, sin_table):
    half_dim = HEAD_FEATURES // 2
    a, b = vectors[..., :half_dim], vectors[..., half_dim:]
    cos_wide, sin_wide = cos_table[:, None, :], sin_table[:, None, :]
    return jnp.concatenate([a * cos_wide - b * sin_wide, b * cos_wide + a * sin_wide], axis=-1)


def unrotate(vectors, cos_table, sin_table):
    return rotate(vectors, cos_table, -sin_table)


def wide_dot(a, b):
    return jnp.dot(a, b, preferred_element_type=jnp.float32)


def dot_last(a, b):
    return lax.dot_general(a, b, (((1,), (1,)), ((), ())), preferred_element_type=jnp.float32)


def dot_first(a, b):
    return lax.dot_general(a, b, (((0,), (0,)), ((), ())), preferred_element_type=jnp.float32)


def pad_lanes(parts, rows):
    joined = jnp.concatenate(parts, axis=1)
    missing = -joined.shape[1] % 128
    return jnp.concatenate([joined, jnp.zeros((rows, missing), joined.dtype)], axis=1)


def high_low(values):
    high = values.astype(jnp.bfloat16)
    return [high, (values - high.astype(jnp.float32)).astype(jnp.bfloat16)]


def on_device(
    hidden_in,
    segments,
    routes,
    attn_gain,
    w_query,
    key_projection,
    value_projection,
    w_out,
    moe_gain,
    w_router,
    w_gate,
    w_up,
    w_down,
    out_grad,
):
    seq_rows = hidden_in.shape[1]
    model_width = hidden_in.shape[2]
    quarter = routes.shape[1]
    expert_count = w_router.shape[1]
    tensor_rank = lax.axis_index("tensor")
    context_rank = lax.axis_index("context")
    fsdp_size, context_size, tensor_size = (
        lax.axis_size("fsdp"),
        lax.axis_size("context"),
        lax.axis_size("tensor"),
    )
    row_count = context_size // 2
    quarter_first = tensor_rank * quarter
    owned = w_query.shape[0]
    q_width, kv_width = w_query.shape[1], key_projection.shape[1]
    out_width = w_out.shape[0]
    seg_columns = seq_rows // owned
    low_segs = segments[0].astype(jnp.bfloat16)
    packed = pad_lanes(
        [
            w_query,
            key_projection,
            value_projection,
            w_out.T,
            w_router,
            attn_gain[:, None],
            moe_gain[:, None],
            low_segs.reshape(seg_columns, owned).T,
        ],
        owned,
    )
    gathered, near_grads = cube_gather(packed, "fsdp", 1, out_grad[0])
    all_small = gathered[..., q_width + 2 * kv_width + out_width :]
    gathered = gathered.reshape(model_width, packed.shape[1])
    qkv_width = q_width + 2 * kv_width
    qkv_w = gathered[:, :qkv_width]
    out_wt = gathered[:, qkv_width : qkv_width + out_width]
    small = gathered[:, qkv_width + out_width :]
    router_w = small[:, :expert_count]
    gain_one = small[:, expert_count].astype(jnp.float32)
    gain_two = small[:, expert_count + 1].astype(jnp.float32)
    fsdp_rank = lax.axis_index("fsdp")
    seq_small = lax.dynamic_index_in_dim(all_small, fsdp_rank, 0, keepdims=False)
    all_segs = (
        seq_small[..., expert_count + 2 : expert_count + 2 + seg_columns]
        .transpose(0, 1, 3, 2)
        .reshape(context_size * seq_rows)
        .astype(jnp.float32)
    )
    gate_full = lax.all_gather(w_gate[0], "fsdp", axis=0, tiled=True)
    up_full = lax.all_gather(w_up[0], "fsdp", axis=0, tiled=True)
    down_full = lax.all_gather(w_down[0], "fsdp", axis=1, tiled=True)

    hidden = hidden_in[0].astype(jnp.float32)
    scale_one = norm_scale(hidden)
    unit_one = hidden * scale_one
    normed_input = (unit_one * gain_one).astype(jnp.bfloat16)
    positions = context_rank * seq_rows + jnp.arange(seq_rows, dtype=jnp.int32)
    cos_table, sin_table = rope_tables(positions)
    query_heads = q_width // HEAD_FEATURES
    kv_heads = kv_width // HEAD_FEATURES
    group_size = query_heads // kv_heads
    projected = wide_dot(normed_input, qkv_w)
    queries = (
        rotate(
            projected[:, :q_width].reshape(seq_rows, query_heads, HEAD_FEATURES),
            cos_table,
            sin_table,
        )
        * HEAD_FEATURES ** (-0.5)
    ).astype(jnp.bfloat16)
    grouped_queries = queries.reshape(seq_rows, kv_heads, group_size, HEAD_FEATURES)
    keys = (
        rotate(
            projected[:, q_width : q_width + kv_width].reshape(seq_rows, kv_heads, HEAD_FEATURES),
            cos_table,
            sin_table,
        )
        .astype(jnp.bfloat16)
        .reshape(seq_rows, kv_width)
    )
    values = projected[:, q_width + kv_width :].astype(jnp.bfloat16)
    all_kv = axis_gather(jnp.concatenate([keys, values], axis=1), "context", 3)
    total_keys = context_size * seq_rows
    all_kv = all_kv.reshape(total_keys, 2, kv_heads, HEAD_FEATURES)
    all_keys, all_values = all_kv[:, 0], all_kv[:, 1]
    own_seg = segments[0].astype(jnp.float32)
    key_pos = jnp.arange(total_keys, dtype=jnp.int32)
    allowed = (key_pos[None, :] <= positions[:, None]) & (all_segs[None, :] == own_seg[:, None])
    scores = jnp.einsum(
        "rkgd,lkd->kgrl", grouped_queries, all_keys, preferred_element_type=jnp.float32
    )
    scores = jnp.where(allowed, scores, -jnp.inf)
    raised_scores = jnp.exp(scores - jnp.max(scores, axis=-1, keepdims=True))
    probs = raised_scores / jnp.sum(raised_scores, axis=-1, keepdims=True)
    probs_low = probs.astype(jnp.bfloat16)
    mixed = (
        jnp.einsum("kgrl,lkd->rkgd", probs_low, all_values, preferred_element_type=jnp.float32)
        .astype(jnp.bfloat16)
        .reshape(seq_rows, q_width)
    )
    attn_part = dot_last(mixed, out_wt).astype(jnp.bfloat16)
    attn_out, all_out_grad = scatter_and_spread(
        attn_part.reshape(tensor_size, quarter, model_width), near_grads, 4
    )
    all_out_grad = all_out_grad.reshape(-1, model_width)
    res_rows = lax.dynamic_slice_in_dim(hidden, quarter_first, quarter, 0) + attn_out
    scale_two = norm_scale(res_rows)
    unit_two = res_rows * scale_two
    normed_two = (unit_two * gain_two).astype(jnp.bfloat16)
    logits = wide_dot(normed_two, router_w)
    named = jnp.any(
        routes[0][:, :, None] == jnp.arange(expert_count, dtype=jnp.int32)[None, None, :], axis=1
    )
    top_logit = jnp.max(jnp.where(named, logits, -jnp.inf), axis=-1, keepdims=True)
    raised = jnp.where(named, jnp.exp(jnp.where(named, logits - top_logit, 0.0)), 0.0)
    gate_weight = raised / jnp.sum(raised, axis=-1, keepdims=True)
    sent = pad_lanes([normed_two] + high_low(gate_weight), quarter)
    arrived = cube_gather(sent, "tensor", 5).reshape(-1, sent.shape[1])
    own_expert = (context_rank * tensor_size + tensor_rank).astype(jnp.int32).reshape(1)
    returned, weighted_out, expert_terms = expert_pass(
        own_expert, arrived, all_out_grad, gate_full, up_full, down_full, expert_count
    )
    summed = cube_scatter(
        returned.reshape(tensor_size, row_count, 2, quarter, returned.shape[1]), "tensor", 6
    )
    picks = (
        summed[:, model_width : model_width + expert_count]
        + summed[:, model_width + expert_count : model_width + 2 * expert_count]
    )
    logit_grads = (
        gate_weight * (picks - jnp.sum(gate_weight * picks, axis=-1, keepdims=True))
    ).astype(jnp.bfloat16)
    router_part = dot_first(normed_two, logit_grads)
    norm_two_grads = summed[:, :model_width] + dot_last(logit_grads, router_w)

    expert_grads = lax.psum_scatter(expert_terms, "fsdp", scatter_dimension=0, tiled=True).astype(
        jnp.float32
    )
    hidden_units = w_gate.shape[2]
    gate_grad = expert_grads[None, :, :hidden_units]
    up_grad = expert_grads[None, :, hidden_units : 2 * hidden_units]
    down_grad = expert_grads[:, 2 * hidden_units :].T[None]

    grad_rows = out_grad[0].astype(jnp.float32)
    scaled_grads = norm_two_grads * gain_two
    gain_two_part = jnp.sum(norm_two_grads * unit_two, axis=0)
    res_grads = grad_rows + scale_two * (
        scaled_grads - unit_two * jnp.mean(scaled_grads * unit_two, axis=-1, keepdims=True)
    )
    attn_grads, folded_out = gather_and_fold(
        res_grads.astype(jnp.bfloat16),
        weighted_out.reshape(tensor_size, row_count, 2, quarter, model_width),
        7,
    )
    attn_grads = attn_grads.reshape(seq_rows, model_width)
    out_term = dot_first(attn_grads, mixed)
    mixed_grads = (
        wide_dot(attn_grads, out_wt)
        .astype(jnp.bfloat16)
        .reshape(seq_rows, kv_heads, group_size, HEAD_FEATURES)
    )
    prob_grads = jnp.einsum(
        "rkgd,lkd->kgrl", mixed_grads, all_values, preferred_element_type=jnp.float32
    )
    delta = jnp.sum(probs * prob_grads, axis=-1, keepdims=True)
    score_grads = (probs * (prob_grads - delta)).astype(jnp.bfloat16)
    query_sums = jnp.einsum(
        "kgrl,lkd->rkgd", score_grads, all_keys, preferred_element_type=jnp.float32
    )
    key_terms = jnp.einsum(
        "kgrl,rkgd->lkd", score_grads, grouped_queries, preferred_element_type=jnp.float32
    )
    value_terms = jnp.einsum(
        "kgrl,rkgd->lkd", probs_low, mixed_grads, preferred_element_type=jnp.float32
    )
    kv_terms = jnp.concatenate(
        [key_terms.reshape(total_keys, kv_width), value_terms.reshape(total_keys, kv_width)], axis=1
    ).astype(jnp.bfloat16)
    kv_sums = axis_scatter(
        kv_terms.reshape(context_size, seq_rows, 2 * kv_width), "context", 8, jnp.float32
    )
    key_grads = unrotate(
        kv_sums[:, :kv_width].reshape(seq_rows, kv_heads, HEAD_FEATURES), cos_table, sin_table
    ).reshape(seq_rows, kv_width)
    query_grads = unrotate(
        query_sums.reshape(seq_rows, query_heads, HEAD_FEATURES) * HEAD_FEATURES ** (-0.5),
        cos_table,
        sin_table,
    ).reshape(seq_rows, q_width)
    qkv_grads = jnp.concatenate([query_grads, key_grads, kv_sums[:, kv_width:]], axis=1).astype(
        jnp.bfloat16
    )
    normed_part = dot_last(qkv_grads, qkv_w).astype(jnp.bfloat16)
    qkv_term = dot_first(normed_input, qkv_grads)
    normed_grads = axis_scatter(
        normed_part.reshape(tensor_size, quarter, model_width), "tensor", 9, jnp.float32
    )
    own_unit = lax.dynamic_slice_in_dim(unit_one, quarter_first, quarter, 0)
    own_scale = lax.dynamic_slice_in_dim(scale_one, quarter_first, quarter, 0)
    scaled_one = normed_grads * gain_one
    gain_one_part = jnp.sum(normed_grads * own_unit, axis=0)
    input_grad = (
        res_grads
        + own_scale
        * (scaled_one - own_unit * jnp.mean(scaled_one * own_unit, axis=-1, keepdims=True))
    )[None]
    terms = pad_lanes(
        [qkv_term, out_term, router_part, gain_one_part[:, None], gain_two_part[:, None]],
        model_width,
    ).astype(jnp.bfloat16)
    sums, moe_out = cube_scatter(
        terms.reshape(fsdp_size, row_count, 2, owned, terms.shape[1]),
        "fsdp",
        10,
        folded_out,
        qkv_width + out_width,
    )
    shared = sums[:, qkv_width + out_width :]
    block_output = (res_rows + moe_out).astype(jnp.bfloat16)[None]
    return (
        block_output,
        input_grad,
        shared[:, expert_count],
        sums[:, :q_width],
        sums[:, q_width : q_width + kv_width],
        sums[:, q_width + kv_width : qkv_width],
        sums[:, qkv_width : qkv_width + out_width].T,
        shared[:, expert_count + 1],
        shared[:, :expert_count],
        gate_grad,
        up_grad,
        down_grad,
    )


def solution(mesh):
    return jax.shard_map(
        on_device,
        mesh=mesh,
        in_specs=(
            P("fsdp", "context", None),
            P("fsdp", "context"),
            P("fsdp", ("context", "tensor"), None),
            P(("fsdp", "context")),
            P(("fsdp", "context"), "tensor"),
            P(("fsdp", "context"), "tensor"),
            P(("fsdp", "context"), "tensor"),
            P("tensor", ("fsdp", "context")),
            P(("fsdp", "context")),
            P(("fsdp", "context"), None),
            P(("context", "tensor"), "fsdp", None),
            P(("context", "tensor"), "fsdp", None),
            P(("context", "tensor"), None, "fsdp"),
            P("fsdp", ("context", "tensor"), None),
        ),
        out_specs=(
            P("fsdp", ("context", "tensor"), None),
            P("fsdp", ("context", "tensor"), None),
            P(("fsdp", "context")),
            P(("fsdp", "context"), "tensor"),
            P(("fsdp", "context"), "tensor"),
            P(("fsdp", "context"), "tensor"),
            P("tensor", ("fsdp", "context")),
            P(("fsdp", "context")),
            P(("fsdp", "context"), None),
            P(("context", "tensor"), "fsdp", None),
            P(("context", "tensor"), "fsdp", None),
            P(("context", "tensor"), None, "fsdp"),
        ),
        check_vma=False,
    )
```

```python
import functools

import jax
import jax.numpy as jnp
from jax import lax
from jax.experimental import pallas as pl
from jax.experimental.pallas import tpu as pltpu
from jax.sharding import PartitionSpec as P

HEAD_FEATURES = 64
rope_base = 10000.0
norm_eps = 1e-06
MESH = pl.DeviceIdType.MESH
VMEM_LIMIT = 48 * 1024 * 1024


def wrap(value, size):
    return lax.rem(value + size, size)


def greet(devices):
    barrier = pltpu.get_barrier_semaphore()
    for device in devices:
        pl.semaphore_signal(barrier, inc=1, device_id=device, device_id_type=MESH)
    pl.semaphore_wait(barrier, len(devices))


def send(source, target, send_sem, recv_sem, device):
    copy = pltpu.make_async_remote_copy(
        src_ref=source,
        dst_ref=target,
        send_sem=send_sem,
        recv_sem=recv_sem,
        device_id=device,
        device_id_type=MESH,
    )
    copy.start()
    return copy


def axis_gather_kernel(axis, size, x_ref, o_ref, send_sem, recv_sem, own_sem):
    me = lax.axis_index(axis)
    peers = [{axis: wrap(me + k, size)} for k in range(1, size)]
    greet(peers)
    copies = [
        send(x_ref, o_ref.at[me], send_sem.at[k], recv_sem.at[k], peers[k]) for k in range(size - 1)
    ]
    own = pltpu.make_async_copy(x_ref, o_ref.at[me], own_sem)
    own.start()
    own.wait()
    for copy in copies:
        copy.wait()


def axis_gather(x, axis, number):
    size = lax.axis_size(axis)
    return pl.pallas_call(
        functools.partial(axis_gather_kernel, axis, size),
        out_shape=jax.ShapeDtypeStruct((size,) + x.shape, x.dtype),
        in_specs=[pl.BlockSpec(memory_space=pltpu.VMEM)],
        out_specs=pl.BlockSpec(memory_space=pltpu.VMEM),
        scratch_shapes=[
            pltpu.SemaphoreType.DMA((size - 1,)),
            pltpu.SemaphoreType.DMA((size - 1,)),
            pltpu.SemaphoreType.DMA,
        ],
        compiler_params=pltpu.CompilerParams(
            collective_id=number, has_side_effects=True, vmem_limit_bytes=VMEM_LIMIT
        ),
        name="axis_gather_%d" % number,
    )(x)


def two_scatter_kernel(sizes, x_ref, y_ref, o_ref, z_ref, h1, h2, s1, r1, s2, r2):
    jobs = [
        ("context", sizes[0], x_ref, o_ref, h1, s1, r1),
        ("tensor", sizes[1], y_ref, z_ref, h2, s2, r2),
    ]
    peers = []
    for axis, size, *rest in jobs:
        peers += [{axis: wrap(lax.axis_index(axis) + k, size)} for k in range(1, size)]
    greet(peers)
    started = []
    for axis, size, source, target, held, sent, got in jobs:
        places = [wrap(lax.axis_index(axis) + k, size) for k in range(1, size)]
        started.append(
            [
                send(source.at[places[k]], held.at[k], sent.at[k], got.at[k], {axis: places[k]})
                for k in range(size - 1)
            ]
        )
    for copies, (axis, size, source, target, held, sent, got) in zip(started, jobs):
        for copy in copies:
            copy.wait()
        total = source[lax.axis_index(axis)].astype(jnp.float32)
        for k in range(size - 1):
            total = total + held[k].astype(jnp.float32)
        target[...] = total


def two_scatter(x, y, number):
    sizes = (lax.axis_size("context"), lax.axis_size("tensor"))
    vmem = pl.BlockSpec(memory_space=pltpu.VMEM)
    several = [pltpu.SemaphoreType.DMA((size - 1,)) for size in sizes]
    return pl.pallas_call(
        functools.partial(two_scatter_kernel, sizes),
        out_shape=[
            jax.ShapeDtypeStruct(x.shape[1:], jnp.float32),
            jax.ShapeDtypeStruct(y.shape[1:], jnp.float32),
        ],
        in_specs=[vmem] * 2,
        out_specs=[vmem] * 2,
        scratch_shapes=[
            pltpu.VMEM((sizes[0] - 1,) + x.shape[1:], x.dtype),
            pltpu.VMEM((sizes[1] - 1,) + y.shape[1:], y.dtype),
            several[0],
            several[0],
            several[1],
            several[1],
        ],
        compiler_params=pltpu.CompilerParams(
            collective_id=number, has_side_effects=True, vmem_limit_bytes=VMEM_LIMIT
        ),
        name="two_scatter_%d" % number,
    )(x, y)


def cube_places(axis, outer, rows):
    a = lax.axis_index(axis)
    context = lax.axis_index("context")
    x, c = context // 2, lax.rem(context, 2)
    outer_places = [wrap(a + k, outer) for k in range(outer)]
    row_places = [wrap(x + j, rows) for j in range(rows)]
    outer_peers = [{axis: place} for place in outer_places]
    row_peers = [{"context": place * 2 + c} for place in row_places]
    core_peer = {"context": x * 2 + (1 - c)}
    return a, x, c, outer_places, row_places, outer_peers, row_peers, core_peer


def cube_gather_kernel(axis, outer, rows, pieces, beside, *refs):
    if beside:
        x_ref, y_ref, o_ref, z_ref, s1, r1, s2, r2, s3, r3, own_sem, s4, r4, own_y = refs
    else:
        x_ref, o_ref, s1, r1, s2, r2, s3, r3, own_sem = refs
    a, x, c, outer_places, row_places, outer_peers, row_peers, core_peer = cube_places(
        axis, outer, rows
    )
    side_peers = []
    if beside:
        me = lax.axis_index("tensor")
        side_peers = [{"tensor": wrap(me + k, beside)} for k in range(1, beside)]
    greet(outer_peers[1:] + row_peers[1:] + [core_peer] + side_peers)
    own = pltpu.make_async_copy(x_ref, o_ref.at[a, x, c], own_sem)
    own.start()
    height = x_ref.shape[0] // pieces
    spans = [pl.ds(p * height, height) for p in range(pieces)]
    first, second, third, side = {}, {}, {}, []
    for p in range(pieces):
        for k in range(1, outer):
            first[p, k] = send(
                x_ref.at[spans[p]],
                o_ref.at[a, x, c, spans[p]],
                s1.at[p, k],
                r1.at[p, k],
                outer_peers[k],
            )
    if beside:
        own_side = pltpu.make_async_copy(y_ref, z_ref.at[me], own_y)
        own_side.start()
        side = [
            send(y_ref, z_ref.at[me], s4.at[k], r4.at[k], side_peers[k]) for k in range(beside - 1)
        ]
    own.wait()
    blocks = [(p, 0) for p in range(pieces)]
    blocks += [(p, k) for p in range(pieces) for k in range(1, outer)]
    for p, k in blocks:
        if k:
            first[p, k].wait_recv()
        held = o_ref.at[wrap(a - k, outer), x, c, spans[p]]
        for j in range(1, rows):
            second[p, k, j] = send(held, held, s2.at[p, k, j], r2.at[p, k, j], row_peers[j])
        third[p, k, 0] = send(held, held, s3.at[p, k, 0], r3.at[p, k, 0], core_peer)
    for p, k in blocks:
        for j in range(1, rows):
            second[p, k, j].wait_recv()
            held = o_ref.at[wrap(a - k, outer), wrap(x - j, rows), c, spans[p]]
            third[p, k, j] = send(held, held, s3.at[p, k, j], r3.at[p, k, j], core_peer)
    for copy in third.values():
        copy.wait_recv()
    for copy in list(first.values()) + list(second.values()) + list(third.values()):
        copy.wait_send()
    if beside:
        own_side.wait()
    for copy in side:
        copy.wait()


def cube_gather(x, axis, number, beside=None):
    outer, rows = lax.axis_size(axis), lax.axis_size("context") // 2
    pieces = 2 if x.shape[0] % 32 == 0 else 1
    single = pltpu.SemaphoreType.DMA((pieces, outer))
    pair = pltpu.SemaphoreType.DMA((pieces, outer, rows))
    vmem = pl.BlockSpec(memory_space=pltpu.VMEM)
    shapes = [jax.ShapeDtypeStruct((outer, rows, 2) + x.shape, x.dtype)]
    scratch = [single, single, pair, pair, pair, pair, pltpu.SemaphoreType.DMA]
    args = [x]
    side = 0
    if beside is not None:
        side = lax.axis_size("tensor")
        args.append(beside)
        shapes.append(jax.ShapeDtypeStruct((side,) + beside.shape, beside.dtype))
        several = pltpu.SemaphoreType.DMA((side - 1,))
        scratch += [several, several, pltpu.SemaphoreType.DMA]
    outs = pl.pallas_call(
        functools.partial(cube_gather_kernel, axis, outer, rows, pieces, side),
        out_shape=shapes,
        in_specs=[vmem] * len(args),
        out_specs=[vmem] * len(shapes),
        scratch_shapes=scratch,
        compiler_params=pltpu.CompilerParams(
            collective_id=number, has_side_effects=True, vmem_limit_bytes=VMEM_LIMIT
        ),
        name="cube_gather_%d" % number,
    )(*args)
    return outs if beside is not None else outs[0]


def scatter_and_spread_kernel(
    size, rows, x_ref, y_ref, o_ref, z_ref, held, s1, r1, s2, r2, s3, r3, own_sem
):
    a, x, c, places, row_places, peers, row_peers, core_peer = cube_places("tensor", size, rows)
    greet(peers[1:] + row_peers[1:] + [core_peer])
    first = [
        send(x_ref.at[places[k]], held.at[k - 1], s1.at[k], r1.at[k], peers[k])
        for k in range(1, size)
    ]
    own = [
        pltpu.make_async_copy(y_ref.at[k], z_ref.at[k, x, c], own_sem.at[k]) for k in range(size)
    ]
    for copy in own:
        copy.start()
    second, third = {}, {}
    for k in range(size):
        for j in range(1, rows):
            second[k, j] = send(
                y_ref.at[k], z_ref.at[k, x, c], s2.at[k, j], r2.at[k, j], row_peers[j]
            )
        third[k, 0] = send(y_ref.at[k], z_ref.at[k, x, c], s3.at[k, 0], r3.at[k, 0], core_peer)
    for k in range(size):
        for j in range(1, rows):
            second[k, j].wait_recv()
            block = z_ref.at[k, wrap(x - j, rows), c]
            third[k, j] = send(block, block, s3.at[k, j], r3.at[k, j], core_peer)
    for copy in first:
        copy.wait()
    total = x_ref[a].astype(jnp.float32)
    for k in range(size - 1):
        total = total + held[k].astype(jnp.float32)
    o_ref[...] = total
    for copy in own:
        copy.wait()
    for copy in second.values():
        copy.wait_send()
    for copy in third.values():
        copy.wait()


def scatter_and_spread(x, y, number):
    size, rows = lax.axis_size("tensor"), lax.axis_size("context") // 2
    vmem = pl.BlockSpec(memory_space=pltpu.VMEM)
    several = pltpu.SemaphoreType.DMA((size,))
    pair = pltpu.SemaphoreType.DMA((size, rows))
    return pl.pallas_call(
        functools.partial(scatter_and_spread_kernel, size, rows),
        out_shape=[
            jax.ShapeDtypeStruct(x.shape[1:], jnp.float32),
            jax.ShapeDtypeStruct((size, rows, 2) + y.shape[1:], y.dtype),
        ],
        in_specs=[vmem] * 2,
        out_specs=[vmem] * 2,
        scratch_shapes=[
            pltpu.VMEM((size - 1,) + x.shape[1:], x.dtype),
            several,
            several,
            pair,
            pair,
            pair,
            pair,
            several,
        ],
        compiler_params=pltpu.CompilerParams(
            collective_id=number, has_side_effects=True, vmem_limit_bytes=VMEM_LIMIT
        ),
        name="scatter_and_spread_%d" % number,
    )(x, y)


def gather_and_fold_kernel(
    size, rows, x_ref, y_ref, o_ref, z_ref, h1, part, h2, s1, r1, s2, r2, s3, r3, own_sem
):
    a, x, c, places, row_places, peers, row_peers, core_peer = cube_places("tensor", size, rows)
    greet(peers[1:] + row_peers[1:] + [core_peer])
    first = [
        send(x_ref, o_ref.at[a], s1.at[k], r1.at[k], peers[k]) for k in range(1, size)
    ]
    own = pltpu.make_async_copy(x_ref, o_ref.at[a], own_sem)
    own.start()
    order = [(k, j) for j in reversed(range(rows)) for k in range(size)]
    second, third = {}, {}
    for k, j in order:
        place = row_places[j]
        second[k, j] = send(
            y_ref.at[k, place, 1 - c], h1.at[k, place], s2.at[k, j], r2.at[k, j], core_peer
        )
    for k, j in order:
        place = row_places[j]
        second[k, j].wait_recv()
        total = y_ref[k, place, c].astype(jnp.float32) + h1[k, place].astype(jnp.float32)
        part[k, j] = total.astype(part.dtype)
        if j:
            third[k, j] = send(part.at[k, j], h2.at[k, j], s3.at[k, j], r3.at[k, j], row_peers[j])
    for k in range(size):
        total = part[k, 0].astype(jnp.float32)
        for j in range(1, rows):
            third[k, j].wait_recv()
            total = total + h2[k, j].astype(jnp.float32)
        z_ref[k] = total.astype(z_ref.dtype)
    own.wait()
    for copy in first:
        copy.wait()
    for copy in list(second.values()) + list(third.values()):
        copy.wait_send()


def gather_and_fold(x, y, number):
    size, rows = lax.axis_size("tensor"), lax.axis_size("context") // 2
    vmem = pl.BlockSpec(memory_space=pltpu.VMEM)
    several = pltpu.SemaphoreType.DMA((size,))
    pair = pltpu.SemaphoreType.DMA((size, rows))
    blocks = pltpu.VMEM((size, rows) + y.shape[3:], y.dtype)
    return pl.pallas_call(
        functools.partial(gather_and_fold_kernel, size, rows),
        out_shape=[
            jax.ShapeDtypeStruct((size,) + x.shape, x.dtype),
            jax.ShapeDtypeStruct((size,) + y.shape[3:], y.dtype),
        ],
        in_specs=[vmem] * 2,
        out_specs=[vmem] * 2,
        scratch_shapes=[
            blocks,
            blocks,
            blocks,
            several,
            several,
            pair,
            pair,
            pair,
            pair,
            pltpu.SemaphoreType.DMA,
        ],
        compiler_params=pltpu.CompilerParams(
            collective_id=number, has_side_effects=True, vmem_limit_bytes=VMEM_LIMIT
        ),
        name="gather_and_fold_%d" % number,
    )(x, y)


def expert_kernel(
    experts, chunk, e_ref, tok, grads, wg, wu, wd, rows_o, out_o, terms_o, acc_g, acc_u, acc_d
):
    own = e_ref[0]
    width = grads.shape[1]
    hidden_units = wg.shape[1]
    acc_g[...] = jnp.zeros_like(acc_g)
    acc_u[...] = jnp.zeros_like(acc_u)
    acc_d[...] = jnp.zeros_like(acc_d)
    lane = lax.broadcasted_iota(jnp.int32, (chunk, 128), 1)

    def step(i, carried):
        span = pl.ds(pl.multiple_of(i * chunk, chunk), chunk)
        rows = tok[span, :width]
        table = tok[span, width:].astype(jnp.float32)
        gate = jnp.sum(
            jnp.where((lane == own) | (lane == own + experts), table, 0.0), axis=1, keepdims=True
        )
        wide = grads[span, :].astype(jnp.float32)
        gate_pre = wide_dot(rows, wg[...])
        up_pre = wide_dot(rows, wu[...])
        sig = jax.nn.sigmoid(gate_pre)
        swish = gate_pre * sig
        activated = (swish * up_pre).astype(jnp.bfloat16)
        result = wide_dot(activated, wd[...]).astype(jnp.bfloat16).astype(jnp.float32)
        out_o[span, :] = (gate * result).astype(jnp.bfloat16)
        pick = jnp.sum(wide * result, axis=1, keepdims=True)
        out_grads = (gate * wide).astype(jnp.bfloat16)
        act_grads = dot_last(out_grads, wd[...])
        gate_grads = (act_grads * up_pre * sig * (1.0 + gate_pre * (1.0 - sig))).astype(
            jnp.bfloat16
        )
        up_grads = (act_grads * swish).astype(jnp.bfloat16)
        rows_o[span, :width] = (
            dot_last(gate_grads, wg[...]) + dot_last(up_grads, wu[...])
        ).astype(jnp.bfloat16)
        high = pick.astype(jnp.bfloat16).astype(jnp.float32)
        rows_o[span, width:] = jnp.where(
            lane == own, high, jnp.where(lane == own + experts, pick - high, 0.0)
        ).astype(jnp.bfloat16)
        acc_g[...] += dot_first(rows, gate_grads)
        acc_u[...] += dot_first(rows, up_grads)
        acc_d[...] += dot_first(out_grads, activated)
        return carried

    lax.fori_loop(0, tok.shape[0] // chunk, step, 0)
    terms_o[:, :hidden_units] = acc_g[...].astype(jnp.bfloat16)
    terms_o[:, hidden_units : 2 * hidden_units] = acc_u[...].astype(jnp.bfloat16)
    terms_o[:, 2 * hidden_units :] = acc_d[...].astype(jnp.bfloat16)


def expert_pass(own, tok, grads, wg, wu, wd, experts):
    count, width = grads.shape
    hidden_units = wg.shape[1]
    vmem = pl.BlockSpec(memory_space=pltpu.VMEM)
    return pl.pallas_call(
        functools.partial(expert_kernel, experts, min(256, count)),
        out_shape=[
            jax.ShapeDtypeStruct(tok.shape, jnp.bfloat16),
            jax.ShapeDtypeStruct(grads.shape, jnp.bfloat16),
            jax.ShapeDtypeStruct((width, 3 * hidden_units), jnp.bfloat16),
        ],
        in_specs=[pl.BlockSpec(memory_space=pltpu.SMEM)] + [vmem] * 5,
        out_specs=[vmem] * 3,
        scratch_shapes=[pltpu.VMEM((width, hidden_units), jnp.float32)] * 3,
        compiler_params=pltpu.CompilerParams(vmem_limit_bytes=VMEM_LIMIT),
        name="expert_pass",
    )(own, tok, grads, wg, wu, wd)


def cube_scatter_kernel(axis, outer, rows, pieces, beside, lanes, *refs):
    if beside:
        x_ref, y_ref, o_ref, z_ref = refs[:4]
        h1, part, h2, share, h3, s1, r1, s2, r2, s3, r3 = refs[4:15]
        h4, tail, h5, s4, r4, s5, r5 = refs[15:]
    else:
        x_ref, o_ref, h1, part, h2, share, h3, s1, r1, s2, r2, s3, r3 = refs
    a, x, c, outer_places, row_places, outer_peers, row_peers, core_peer = cube_places(
        axis, outer, rows
    )
    side_peers = []
    if beside:
        me = lax.axis_index("tensor")
        side_places = [wrap(me + k, beside) for k in range(1, beside)]
        side_peers = [{"tensor": place} for place in side_places]
    greet(outer_peers[1:] + row_peers[1:] + [core_peer] + side_peers)
    height = x_ref.shape[3] // pieces
    spans = [pl.ds(p * height, height) for p in range(pieces)]
    order = [
        (p, k, j)
        for p in range(pieces)
        for j in reversed(range(rows))
        for k in reversed(range(outer))
    ]
    first, second, third, side, ends = {}, {}, {}, [], []
    for p, k, j in order:
        first[p, k, j] = send(
            x_ref.at[outer_places[k], row_places[j], 1 - c, spans[p]],
            h1.at[outer_places[k], row_places[j], spans[p]],
            s1.at[p, k, j],
            r1.at[p, k, j],
            core_peer,
        )
    if beside:
        side = [
            send(y_ref.at[side_places[k]], h4.at[k], s4.at[k], r4.at[k], side_peers[k])
            for k in range(beside - 1)
        ]
    for p in range(pieces):
        for j in reversed(range(rows)):
            for k in reversed(range(outer)):
                first[p, k, j].wait_recv()
                block = x_ref[outer_places[k], row_places[j], c, spans[p]].astype(jnp.float32)
                block = block + h1[outer_places[k], row_places[j], spans[p]].astype(jnp.float32)
                part[k, j, spans[p]] = block.astype(part.dtype)
                if j:
                    second[p, k, j] = send(
                        part.at[k, j, spans[p]],
                        h2.at[k, j, spans[p]],
                        s2.at[p, k, j],
                        r2.at[p, k, j],
                        row_peers[j],
                    )
    for p in range(pieces):
        for k in reversed(range(outer)):
            total = part[k, 0, spans[p]].astype(jnp.float32)
            for j in range(1, rows):
                second[p, k, j].wait_recv()
                total = total + h2[k, j, spans[p]].astype(jnp.float32)
            if k:
                share[k, spans[p]] = total.astype(share.dtype)
                third[p, k] = send(
                    share.at[k, spans[p]],
                    h3.at[k, spans[p]],
                    s3.at[p, k],
                    r3.at[p, k],
                    outer_peers[k],
                )
            else:
                o_ref[spans[p]] = total
    for p in range(pieces):
        total = o_ref[spans[p]]
        for k in range(1, outer):
            third[p, k].wait_recv()
            total = total + h3[k, spans[p]].astype(jnp.float32)
        o_ref[spans[p]] = total
    if beside:
        tail[...] = o_ref[:, lanes:].astype(tail.dtype)
        ends = [
            send(tail, h5.at[k], s5.at[k], r5.at[k], side_peers[k]) for k in range(beside - 1)
        ]
        for copy in side:
            copy.wait()
        total = y_ref[me].astype(jnp.float32)
        for k in range(beside - 1):
            total = total + h4[k].astype(jnp.float32)
        z_ref[...] = total
        for copy in ends:
            copy.wait()
        total = o_ref[:, lanes:]
        for k in range(beside - 1):
            total = total + h5[k].astype(jnp.float32)
        o_ref[:, lanes:] = total
    for copy in list(first.values()) + list(second.values()) + list(third.values()):
        copy.wait_send()


def cube_scatter(x, axis, number, beside=None, lanes=0):
    outer, rows = lax.axis_size(axis), lax.axis_size("context") // 2
    block = x.shape[3:]
    pieces = 2 if block[0] % 32 == 0 else 1
    single = pltpu.SemaphoreType.DMA((pieces, outer))
    pair = pltpu.SemaphoreType.DMA((pieces, outer, rows))
    vmem = pl.BlockSpec(memory_space=pltpu.VMEM)
    args = [x]
    shapes = [jax.ShapeDtypeStruct(block, jnp.float32)]
    scratch = [pltpu.VMEM((outer, rows) + block, x.dtype)] * 3
    scratch += [pltpu.VMEM((outer,) + block, x.dtype)] * 2
    scratch += [pair, pair, pair, pair, single, single]
    side = 0
    if beside is not None:
        side = lax.axis_size("tensor")
        args.append(beside)
        shapes.append(jax.ShapeDtypeStruct(beside.shape[1:], jnp.float32))
        several = pltpu.SemaphoreType.DMA((side - 1,))
        tail = (block[0], block[1] - lanes)
        scratch += [
            pltpu.VMEM((side - 1,) + beside.shape[1:], beside.dtype),
            pltpu.VMEM(tail, x.dtype),
            pltpu.VMEM((side - 1,) + tail, x.dtype),
            several,
            several,
            several,
            several,
        ]
    outs = pl.pallas_call(
        functools.partial(cube_scatter_kernel, axis, outer, rows, pieces, side, lanes),
        out_shape=shapes,
        in_specs=[vmem] * len(args),
        out_specs=[vmem] * len(shapes),
        scratch_shapes=scratch,
        compiler_params=pltpu.CompilerParams(
            collective_id=number, has_side_effects=True, vmem_limit_bytes=VMEM_LIMIT
        ),
        name="cube_scatter_%d" % number,
    )(*args)
    return outs if beside is not None else outs[0]


def norm_scale(values):
    return lax.rsqrt(jnp.mean(values * values, axis=-1, keepdims=True) + norm_eps)


def rope_tables(positions):
    half_dim = HEAD_FEATURES // 2
    frequency = rope_base ** (-(2.0 * jnp.arange(half_dim, dtype=jnp.float32)) / HEAD_FEATURES)
    angles = positions.astype(jnp.float32)[:, None] * frequency[None, :]
    return (jnp.cos(angles), jnp.sin(angles))


def rotate(vectors, cos_table, sin_table):
    half_dim = HEAD_FEATURES // 2
    a, b = vectors[..., :half_dim], vectors[..., half_dim:]
    cos_wide, sin_wide = cos_table[:, None, :], sin_table[:, None, :]
    return jnp.concatenate([a * cos_wide - b * sin_wide, b * cos_wide + a * sin_wide], axis=-1)


def unrotate(vectors, cos_table, sin_table):
    return rotate(vectors, cos_table, -sin_table)


def wide_dot(a, b):
    return jnp.dot(a, b, preferred_element_type=jnp.float32)


def dot_last(a, b):
    return lax.dot_general(a, b, (((1,), (1,)), ((), ())), preferred_element_type=jnp.float32)


def dot_first(a, b):
    return lax.dot_general(a, b, (((0,), (0,)), ((), ())), preferred_element_type=jnp.float32)


def pad_lanes(parts, rows):
    joined = jnp.concatenate(parts, axis=1)
    missing = -joined.shape[1] % 128
    return jnp.concatenate([joined, jnp.zeros((rows, missing), joined.dtype)], axis=1)


def high_low(values):
    high = values.astype(jnp.bfloat16)
    return [high, (values - high.astype(jnp.float32)).astype(jnp.bfloat16)]


def on_device(
    hidden_in,
    segments,
    routes,
    attn_gain,
    w_query,
    key_projection,
    value_projection,
    w_out,
    moe_gain,
    w_router,
    w_gate,
    w_up,
    w_down,
    out_grad,
):
    seq_rows = hidden_in.shape[1]
    model_width = hidden_in.shape[2]
    quarter = routes.shape[1]
    expert_count = w_router.shape[1]
    tensor_rank = lax.axis_index("tensor")
    context_rank = lax.axis_index("context")
    fsdp_size, context_size, tensor_size = (
        lax.axis_size("fsdp"),
        lax.axis_size("context"),
        lax.axis_size("tensor"),
    )
    row_count = context_size // 2
    quarter_first = tensor_rank * quarter
    owned = w_query.shape[0]
    q_width, kv_width = w_query.shape[1], key_projection.shape[1]
    out_width = w_out.shape[0]
    seg_columns = seq_rows // owned
    low_segs = segments[0].astype(jnp.bfloat16)
    packed = pad_lanes(
        [
            w_query,
            key_projection,
            value_projection,
            w_out.T,
            w_router,
            attn_gain[:, None],
            moe_gain[:, None],
            low_segs.reshape(seg_columns, owned).T,
        ],
        owned,
    )
    gathered, near_grads = cube_gather(packed, "fsdp", 1, out_grad[0])
    all_small = gathered[..., q_width + 2 * kv_width + out_width :]
    gathered = gathered.reshape(model_width, packed.shape[1])
    qkv_width = q_width + 2 * kv_width
    qkv_w = gathered[:, :qkv_width]
    out_wt = gathered[:, qkv_width : qkv_width + out_width]
    small = gathered[:, qkv_width + out_width :]
    router_w = small[:, :expert_count]
    gain_one = small[:, expert_count].astype(jnp.float32)
    gain_two = small[:, expert_count + 1].astype(jnp.float32)
    fsdp_rank = lax.axis_index("fsdp")
    seq_small = lax.dynamic_index_in_dim(all_small, fsdp_rank, 0, keepdims=False)
    all_segs = (
        seq_small[..., expert_count + 2 : expert_count + 2 + seg_columns]
        .transpose(0, 1, 3, 2)
        .reshape(context_size * seq_rows)
        .astype(jnp.float32)
    )
    gate_full = lax.all_gather(w_gate[0], "fsdp", axis=0, tiled=True)
    up_full = lax.all_gather(w_up[0], "fsdp", axis=0, tiled=True)
    down_full = lax.all_gather(w_down[0], "fsdp", axis=1, tiled=True)

    hidden = hidden_in[0].astype(jnp.float32)
    scale_one = norm_scale(hidden)
    unit_one = hidden * scale_one
    normed_input = (unit_one * gain_one).astype(jnp.bfloat16)
    positions = context_rank * seq_rows + jnp.arange(seq_rows, dtype=jnp.int32)
    cos_table, sin_table = rope_tables(positions)
    query_heads = q_width // HEAD_FEATURES
    kv_heads = kv_width // HEAD_FEATURES
    group_size = query_heads // kv_heads
    projected = wide_dot(normed_input, qkv_w)
    queries = (
        rotate(
            projected[:, :q_width].reshape(seq_rows, query_heads, HEAD_FEATURES),
            cos_table,
            sin_table,
        )
        * HEAD_FEATURES ** (-0.5)
    ).astype(jnp.bfloat16)
    grouped_queries = queries.reshape(seq_rows, kv_heads, group_size, HEAD_FEATURES)
    keys = (
        rotate(
            projected[:, q_width : q_width + kv_width].reshape(seq_rows, kv_heads, HEAD_FEATURES),
            cos_table,
            sin_table,
        )
        .astype(jnp.bfloat16)
        .reshape(seq_rows, kv_width)
    )
    values = projected[:, q_width + kv_width :].astype(jnp.bfloat16)
    all_kv = axis_gather(jnp.concatenate([keys, values], axis=1), "context", 3)
    total_keys = context_size * seq_rows
    all_kv = all_kv.reshape(total_keys, 2, kv_heads, HEAD_FEATURES)
    all_keys, all_values = all_kv[:, 0], all_kv[:, 1]
    own_seg = segments[0].astype(jnp.float32)
    key_pos = jnp.arange(total_keys, dtype=jnp.int32)
    allowed = (key_pos[None, :] <= positions[:, None]) & (all_segs[None, :] == own_seg[:, None])
    scores = jnp.einsum(
        "rkgd,lkd->kgrl", grouped_queries, all_keys, preferred_element_type=jnp.float32
    )
    scores = jnp.where(allowed, scores, -jnp.inf)
    raised_scores = jnp.exp(scores - jnp.max(scores, axis=-1, keepdims=True))
    probs = raised_scores / jnp.sum(raised_scores, axis=-1, keepdims=True)
    probs_low = probs.astype(jnp.bfloat16)
    mixed = (
        jnp.einsum("kgrl,lkd->rkgd", probs_low, all_values, preferred_element_type=jnp.float32)
        .astype(jnp.bfloat16)
        .reshape(seq_rows, q_width)
    )
    attn_part = dot_last(mixed, out_wt).astype(jnp.bfloat16)
    attn_out, all_out_grad = scatter_and_spread(
        attn_part.reshape(tensor_size, quarter, model_width), near_grads, 4
    )
    all_out_grad = all_out_grad.reshape(-1, model_width)
    res_rows = lax.dynamic_slice_in_dim(hidden, quarter_first, quarter, 0) + attn_out
    scale_two = norm_scale(res_rows)
    unit_two = res_rows * scale_two
    normed_two = (unit_two * gain_two).astype(jnp.bfloat16)
    logits = wide_dot(normed_two, router_w)
    named = jnp.any(
        routes[0][:, :, None] == jnp.arange(expert_count, dtype=jnp.int32)[None, None, :], axis=1
    )
    top_logit = jnp.max(jnp.where(named, logits, -jnp.inf), axis=-1, keepdims=True)
    raised = jnp.where(named, jnp.exp(jnp.where(named, logits - top_logit, 0.0)), 0.0)
    gate_weight = raised / jnp.sum(raised, axis=-1, keepdims=True)
    sent = pad_lanes([normed_two] + high_low(gate_weight), quarter)
    arrived = cube_gather(sent, "tensor", 5).reshape(-1, sent.shape[1])
    own_expert = (context_rank * tensor_size + tensor_rank).astype(jnp.int32).reshape(1)
    returned, weighted_out, expert_terms = expert_pass(
        own_expert, arrived, all_out_grad, gate_full, up_full, down_full, expert_count
    )
    summed = cube_scatter(
        returned.reshape(tensor_size, row_count, 2, quarter, returned.shape[1]), "tensor", 6
    )
    picks = (
        summed[:, model_width : model_width + expert_count]
        + summed[:, model_width + expert_count : model_width + 2 * expert_count]
    )
    logit_grads = (
        gate_weight * (picks - jnp.sum(gate_weight * picks, axis=-1, keepdims=True))
    ).astype(jnp.bfloat16)
    router_part = dot_first(normed_two, logit_grads)
    norm_two_grads = summed[:, :model_width] + dot_last(logit_grads, router_w)

    expert_grads = lax.psum_scatter(expert_terms, "fsdp", scatter_dimension=0, tiled=True).astype(
        jnp.float32
    )
    hidden_units = w_gate.shape[2]
    gate_grad = expert_grads[None, :, :hidden_units]
    up_grad = expert_grads[None, :, hidden_units : 2 * hidden_units]
    down_grad = expert_grads[:, 2 * hidden_units :].T[None]

    grad_rows = out_grad[0].astype(jnp.float32)
    scaled_grads = norm_two_grads * gain_two
    gain_two_part = jnp.sum(norm_two_grads * unit_two, axis=0)
    res_grads = grad_rows + scale_two * (
        scaled_grads - unit_two * jnp.mean(scaled_grads * unit_two, axis=-1, keepdims=True)
    )
    attn_grads, folded_out = gather_and_fold(
        res_grads.astype(jnp.bfloat16),
        weighted_out.reshape(tensor_size, row_count, 2, quarter, model_width),
        7,
    )
    attn_grads = attn_grads.reshape(seq_rows, model_width)
    out_term = dot_first(attn_grads, mixed)
    mixed_grads = (
        wide_dot(attn_grads, out_wt)
        .astype(jnp.bfloat16)
        .reshape(seq_rows, kv_heads, group_size, HEAD_FEATURES)
    )
    prob_grads = jnp.einsum(
        "rkgd,lkd->kgrl", mixed_grads, all_values, preferred_element_type=jnp.float32
    )
    delta = jnp.sum(probs * prob_grads, axis=-1, keepdims=True)
    score_grads = (probs * (prob_grads - delta)).astype(jnp.bfloat16)
    query_sums = jnp.einsum(
        "kgrl,lkd->rkgd", score_grads, all_keys, preferred_element_type=jnp.float32
    )
    key_terms = jnp.einsum(
        "kgrl,rkgd->lkd", score_grads, grouped_queries, preferred_element_type=jnp.float32
    )
    value_terms = jnp.einsum(
        "kgrl,rkgd->lkd", probs_low, mixed_grads, preferred_element_type=jnp.float32
    )
    kv_terms = jnp.concatenate(
        [key_terms.reshape(total_keys, kv_width), value_terms.reshape(total_keys, kv_width)], axis=1
    ).astype(jnp.bfloat16)
    kv_sums, moe_out = two_scatter(
        kv_terms.reshape(context_size, seq_rows, 2 * kv_width), folded_out, 8
    )
    block_output = (res_rows + moe_out).astype(jnp.bfloat16)[None]
    key_grads = unrotate(
        kv_sums[:, :kv_width].reshape(seq_rows, kv_heads, HEAD_FEATURES), cos_table, sin_table
    ).reshape(seq_rows, kv_width)
    query_grads = unrotate(
        query_sums.reshape(seq_rows, query_heads, HEAD_FEATURES) * HEAD_FEATURES ** (-0.5),
        cos_table,
        sin_table,
    ).reshape(seq_rows, q_width)
    qkv_grads = jnp.concatenate([query_grads, key_grads, kv_sums[:, kv_width:]], axis=1).astype(
        jnp.bfloat16
    )
    normed_wide = dot_last(qkv_grads, qkv_w)
    normed_part = normed_wide.astype(jnp.bfloat16)
    gain_one_part = jnp.sum(normed_wide * unit_one, axis=0)
    qkv_term = dot_first(normed_input, qkv_grads)
    terms = pad_lanes(
        [qkv_term, out_term, router_part, gain_one_part[:, None], gain_two_part[:, None]],
        model_width,
    ).astype(jnp.bfloat16)
    sums, normed_grads = cube_scatter(
        terms.reshape(fsdp_size, row_count, 2, owned, terms.shape[1]),
        "fsdp",
        10,
        normed_part.reshape(tensor_size, quarter, model_width),
        qkv_width + out_width,
    )
    shared = sums[:, qkv_width + out_width :]
    own_unit = lax.dynamic_slice_in_dim(unit_one, quarter_first, quarter, 0)
    own_scale = lax.dynamic_slice_in_dim(scale_one, quarter_first, quarter, 0)
    scaled_one = normed_grads * gain_one
    input_grad = (
        res_grads
        + own_scale
        * (scaled_one - own_unit * jnp.mean(scaled_one * own_unit, axis=-1, keepdims=True))
    )[None]
    return (
        block_output,
        input_grad,
        shared[:, expert_count],
        sums[:, :q_width],
        sums[:, q_width : q_width + kv_width],
        sums[:, q_width + kv_width : qkv_width],
        sums[:, qkv_width : qkv_width + out_width].T,
        shared[:, expert_count + 1],
        shared[:, :expert_count],
        gate_grad,
        up_grad,
        down_grad,
    )


def solution(mesh):
    return jax.shard_map(
        on_device,
        mesh=mesh,
        in_specs=(
            P("fsdp", "context", None),
            P("fsdp", "context"),
            P("fsdp", ("context", "tensor"), None),
            P(("fsdp", "context")),
            P(("fsdp", "context"), "tensor"),
            P(("fsdp", "context"), "tensor"),
            P(("fsdp", "context"), "tensor"),
            P("tensor", ("fsdp", "context")),
            P(("fsdp", "context")),
            P(("fsdp", "context"), None),
            P(("context", "tensor"), "fsdp", None),
            P(("context", "tensor"), "fsdp", None),
            P(("context", "tensor"), None, "fsdp"),
            P("fsdp", ("context", "tensor"), None),
        ),
        out_specs=(
            P("fsdp", ("context", "tensor"), None),
            P("fsdp", ("context", "tensor"), None),
            P(("fsdp", "context")),
            P(("fsdp", "context"), "tensor"),
            P(("fsdp", "context"), "tensor"),
            P(("fsdp", "context"), "tensor"),
            P("tensor", ("fsdp", "context")),
            P(("fsdp", "context")),
            P(("fsdp", "context"), None),
            P(("context", "tensor"), "fsdp", None),
            P(("context", "tensor"), "fsdp", None),
            P(("context", "tensor"), None, "fsdp"),
        ),
        check_vma=False,
    )
```
